256 devices in a mesh: row: 8 (over y, core), col: 32 (over z, x).
Axes of the slice: x: 4, y: 4, z: 8, core: 2. Of those that a mesh axis runs over, the one named last changes fastest.
Arguments:
- student_image: bfloat16 [16384, 512], P(('row', 'col')), may hold values from -0.16 to 0.16
- student_text: bfloat16 [16384, 512], P(('row', 'col')), may hold values from -0.16 to 0.16
- teacher_image: bfloat16 [16384, 1280], P(('row', 'col')), may hold values from -32 to 32
- teacher_text: bfloat16 [16384, 1280], P(('row', 'col')), may hold values from -32 to 32
- teacher_scale: float32 [], replicated, may hold values from 20 to 250
- student_scale: float32 [], replicated, may hold values from 10 to 250
Outputs:
- image_grad: float32 [16384, 512], P(('row', 'col'))
- text_grad: float32 [16384, 512], P(('row', 'col'))
The draws below stay inside these ranges and needn't reach their ends.
All inputs are finite; a program needn't handle non-finite values.
Results may differ from the reference program's by a relative error of at most 0.012.
The reference program's roundings to bfloat16 on the way (of `weight`) count: a program that leaves them out, or rounds other values in their place, can miss the bound.
Values may be sent and summed in bfloat16 or wider, within the bound.
A program may use at most 64 MiB of HBM per device.

```python
import jax
import jax.numpy as jnp
from jax import lax

DS = 512
DT = 1280
BATCH = 16384


def embedding_rows(key, rows, width, factor):
    own_draw = jnp.clip(jax.random.normal(key, (rows, width), jnp.float32), -8.0, 8.0)
    return (own_draw * factor).astype(jnp.bfloat16)


def draw_teacher_image(key, part):
    key = jax.random.fold_in(key, 1)
    return embedding_rows(key, BATCH, DT, 1.0)


def draw_teacher_text(key, part):
    key = jax.random.fold_in(key, 2)
    return embedding_rows(key, BATCH, DT, 1.0)


def draw_student_image(key, part):
    key = jax.random.fold_in(key, 3)
    return embedding_rows(key, BATCH, DS, 0.005)


def draw_student_text(key, part):
    key = jax.random.fold_in(key, 4)
    return embedding_rows(key, BATCH, DS, 0.005)


def draw_teacher_scale(key, part):
    key = jax.random.fold_in(key, 5)
    return jax.random.uniform(key, (), jnp.float32, 20.0, 100.0)


def draw_student_scale(key, part):
    key = jax.random.fold_in(key, 6)
    return jax.random.uniform(key, (), jnp.float32, 10.0, 60.0)


def setup_inputs(seed: int = 0) -> dict:
    arg_keys = jax.random.split(jax.random.key(seed), 7)
    return {
        "student_image": draw_student_image(jax.random.fold_in(arg_keys[6], 71), 0),
        "student_text": draw_student_text(jax.random.fold_in(arg_keys[6], 71), 0),
        "teacher_image": draw_teacher_image(jax.random.fold_in(arg_keys[6], 71), 0),
        "teacher_text": draw_teacher_text(jax.random.fold_in(arg_keys[6], 71), 0),
        "teacher_scale": draw_teacher_scale(jax.random.fold_in(arg_keys[6], 71), 0),
        "student_scale": draw_student_scale(jax.random.fold_in(arg_keys[6], 71), 0),
    }


EPSILON = 1e-12

def unit_rows(raw):
    values = raw.astype(jnp.float32)
    inverse = lax.rsqrt(lax.optimization_barrier(jnp.sum(values * values, axis=-1, keepdims=True)) + EPSILON)
    return (values * inverse, inverse)

def scaled_logits(left, right, scale):
    product = lax.dot_general(left, right, (((1,), (1,)), ((), ())), precision=lax.Precision.HIGHEST, preferred_element_type=jnp.float32)
    return scale * product

def block_stats(logits, axis):
    peak = lax.optimization_barrier(jnp.max(logits, axis=axis))
    total = lax.optimization_barrier(jnp.sum(jnp.exp(logits - jnp.expand_dims(peak, axis)), axis=axis))
    return (peak, total)

def join_pair(peak_a, total_a, peak_b, total_b):
    top = jnp.maximum(peak_a, peak_b)
    return (top, total_a * jnp.exp(peak_a - top) + total_b * jnp.exp(peak_b - top))

def join_stats(first, second):
    teach_peak, teach_total = join_pair(first[0], first[1], second[0], second[1])
    learn_peak, learn_total = join_pair(first[2], first[3], second[2], second[3])
    return (teach_peak, teach_total, learn_peak, learn_total)

def back_norm(grad, unit, inverse):
    return inverse * (grad - unit * lax.optimization_barrier(jnp.sum(unit * grad, axis=-1, keepdims=True)))

def reference(student_image, student_text, teacher_image, teacher_text, teacher_scale, student_scale):
    image_unit, image_inverse = unit_rows(student_image)
    text_unit, text_inverse = unit_rows(student_text)
    pupil_image = image_unit.astype(jnp.bfloat16)
    pupil_text = text_unit.astype(jnp.bfloat16)
    master_image = unit_rows(teacher_image)[0].astype(jnp.bfloat16)
    master_text = unit_rows(teacher_text)[0].astype(jnp.bfloat16)
    rows_block = min(512, BATCH)
    blocks = BATCH // rows_block
    master_blocks = master_image.astype(jnp.float32).reshape(blocks, rows_block, DT)
    pupil_blocks = pupil_image.astype(jnp.float32).reshape(blocks, rows_block, DS)
    master_cols = master_text.astype(jnp.float32)
    pupil_cols = pupil_text.astype(jnp.float32)

    def first_pass(carried, pieces):
        master_piece, pupil_piece = pieces
        teach = scaled_logits(master_piece, master_cols, teacher_scale)
        learn = scaled_logits(pupil_piece, pupil_cols, student_scale)
        teach_peak, teach_total = block_stats(teach, 0)
        learn_peak, learn_total = block_stats(learn, 0)
        updated = join_stats(carried, (teach_peak, teach_total, learn_peak, learn_total))
        return (updated, block_stats(teach, 1) + block_stats(learn, 1))
    lowest = jnp.full((BATCH,), -jnp.inf, jnp.float32)
    nothing = jnp.zeros((BATCH,), jnp.float32)
    column_stats, row_stats = lax.scan(first_pass, (lowest, nothing, lowest, nothing), (master_blocks, pupil_blocks))

    def second_pass(carried, pieces):
        master_piece, pupil_piece, teach_peak, teach_total, learn_peak, learn_total = pieces
        teach = scaled_logits(master_piece, master_cols, teacher_scale)
        learn = scaled_logits(pupil_piece, pupil_cols, student_scale)
        rows_part = jnp.exp(learn - learn_peak[:, None]) / learn_total[:, None] - jnp.exp(teach - teach_peak[:, None]) / teach_total[:, None]
        cols_part = jnp.exp(learn - column_stats[2][None, :]) / column_stats[3][None, :] - jnp.exp(teach - column_stats[0][None, :]) / column_stats[1][None, :]
        weight = (0.5 * (rows_part + cols_part)).astype(jnp.bfloat16).astype(jnp.float32)
        image_part = student_scale * jnp.dot(weight, pupil_cols, precision=lax.Precision.HIGHEST, preferred_element_type=jnp.float32)
        text_part = student_scale * lax.dot_general(weight, pupil_piece, (((0,), (0,)), ((), ())), precision=lax.Precision.HIGHEST, preferred_element_type=jnp.float32)
        return (carried + text_part, image_part)
    text_unit_grad, image_parts = lax.scan(second_pass, jnp.zeros((BATCH, DS), jnp.float32), (master_blocks, pupil_blocks) + tuple(row_stats))
    image_unit_grad = image_parts.reshape(BATCH, DS)
    return (back_norm(image_unit_grad, image_unit, image_inverse), back_norm(text_unit_grad, text_unit, text_inverse))
```

```python
import functools
import math

import jax
import jax.numpy as jnp
from jax import lax
from jax.experimental import pallas as pl
from jax.experimental.pallas import tpu as pltpu
from jax.sharding import PartitionSpec as P

EPSILON = 1e-12
MESH = pl.DeviceIdType.MESH
NX, NY, NZ = 4, 4, 8
LOG2E = math.log2(math.e)
F32, BF16 = jnp.float32, jnp.bfloat16
COPIES = 160

PAIRS = (
    ((0, 0), (1, 0)),
    ((3, 0), (0, 1)),
    ((0, 3), (2, 0)),
    ((1, 1), (1, 3)),
    ((3, 1), (3, 3)),
    ((2, 1), (2, 3)),
    ((0, 2), (1, 2)),
    ((3, 2), (2, 2)),
)
HALF_BLOCKS = tuple(tuple((h, p, q) for h in (0, 1) for p, q in pair) for pair in PAIRS)
IMAGE_ROW = {key: g * 128 + k * 32 for g, keys in enumerate(HALF_BLOCKS) for k, key in enumerate(keys)}
TEXT_GROUPS = ((1, 7), (2, 6), (3, 5), (0, 4))
TEXT_ROW = {
    (k, sib): g * 256 + sib * 128 + i * 64
    for g, pair in enumerate(TEXT_GROUPS)
    for i, k in enumerate(pair)
    for sib in (0, 1)
}


def unit_rows(raw):
    values = raw.astype(F32)
    inverse = lax.rsqrt(jnp.sum(values * values, axis=-1, keepdims=True) + EPSILON)
    return values * inverse, inverse


def join_lse(parts):
    top = functools.reduce(jnp.maximum, parts)
    total = functools.reduce(jnp.add, [jnp.exp2(part - top) for part in parts])
    return top + jnp.log(total) * LOG2E


def back_norm(grad, raw):
    unit, inverse = unit_rows(raw)
    return inverse * (grad - unit * jnp.sum(unit * grad, axis=-1, keepdims=True))


def nt_dot(a, b):
    return lax.dot_general(a, b, (((1,), (1,)), ((), ())), preferred_element_type=F32)


def tn_dot(a, b):
    return lax.dot_general(a, b, (((0,), (0,)), ((), ())), preferred_element_type=F32)


def kernel(
    tscale_ref, sscale_ref, si_ref, st_ref, ti_ref, tt_ref, image_out, text_out,
    img, txt, teach, learn, weight, row_part, col_part, row_stat, col_stat, row_in, col_in, row_lse, col_lse,
    image_own, image_send, image_in, image_sum, image_send2, image_in2,
    text_own, text_send, text_in, text_send2, text_in2, text_half, text_in3,
    send_sem, recv_sem,
):
    ds = si_ref.shape[1]
    row, col = lax.axis_index("row"), lax.axis_index("col")
    y, core = row // 2, row % 2
    z, x = col // NX, col % NX

    def device(dx=0, dy=0, dz=0, sibling=False):
        c = 1 - core if sibling else core
        return (((y + dy) % NY) * 2 + c, ((z + dz) % NZ) * NX + (x + dx) % NX)

    def along(half, axis, d):
        return device(dx=d) if (half == 0) == (axis == 1) else device(dy=d)

    copies = []

    def send(src, dst, target):
        i = len(copies)
        copy = pltpu.make_async_remote_copy(
            src_ref=src, dst_ref=dst, send_sem=send_sem.at[i], recv_sem=recv_sem.at[i],
            device_id=target, device_id_type=MESH,
        )
        copy.start()
        copies.append(copy)
        return copy

    barrier = pltpu.get_barrier_semaphore()
    peers = [device(dx=d) for d in (1, 2, 3)] + [device(dy=d) for d in (1, 2, 3)]
    peers += [device(dz=d) for d in range(1, NZ)] + [device(sibling=True)]
    for peer in peers:
        pl.semaphore_signal(barrier, inc=1, device_id=peer, device_id_type=MESH)

    own_text = TEXT_ROW[(0, 0)]
    for start, size in ((0, 32), (32, 32)):
        for h_ref, lo, hi in ((si_ref, 0, ds), (ti_ref, ds, img.shape[1])):
            at = IMAGE_ROW[(start // 32, 0, 0)]
            img[at : at + size, lo:hi] = unit_rows(h_ref[start : start + size, :])[0].astype(BF16)
    for h_ref, lo, hi in ((st_ref, 0, ds), (tt_ref, ds, img.shape[1])):
        txt[own_text : own_text + 64, lo:hi] = unit_rows(h_ref[...])[0].astype(BF16)

    pl.semaphore_wait(barrier, len(peers))

    got = {}

    def rows(ref, at, size):
        return ref.at[pl.ds(at, size), :]

    def text_rows(k, h, sib=0):
        return rows(txt, TEXT_ROW[(k, sib)] + h * 32, 32)

    def image_rows(h, p, q, part=None):
        at = IMAGE_ROW[(h, p, q)]
        return rows(img, at, 32) if part is None else rows(img, at + part * 16, 16)

    def to_second_axis(h, p):
        got[h, p, 1] = send(image_rows(h, p, 0), image_rows(h, p, 1), along(h, 2, -1))
        got[h, p, 3] = send(image_rows(h, p, 0), image_rows(h, p, 3), along(h, 2, 1))

    def text_forward(k, h):
        if k in (0, 1, 2):
            got["t", k + 1, h] = send(text_rows(k, h), text_rows(k + 1, h), device(dz=-1))
        if k in (0, 7, 6):
            j = (k + NZ - 1) % NZ
            got["t", j, h] = send(text_rows(k, h), text_rows(j, h), device(dz=1))
        if k == 3 and h == 0:
            got["t", 4, 0] = send(text_rows(3, 0), text_rows(4, 0), device(dz=-1))
        if k == 5 and h == 1:
            got["t", 4, 1] = send(text_rows(5, 1), text_rows(4, 1), device(dz=1))
        got["s", k, h] = send(text_rows(k, h), text_rows(k, h, 1), device(sibling=True))

    def text_arrive(*ks, half):
        for k in ks:
            got["t", k, half].wait_recv()
            text_forward(k, half)

    def first_axis_arrive(p):
        for h in (0, 1):
            got[h, p, 0].wait_recv()
            part = 0 if p == 1 else 1
            d = -1 if p == 1 else 1
            got[h, 2, 0, part] = send(image_rows(h, p, 0, part), image_rows(h, 2, 0, part), along(h, 1, d))
            to_second_axis(h, p)

    def second_axis_arrive(p):
        for h in (0, 1):
            for q, part, d in ((1, 0, -1), (3, 1, 1)):
                got[h, p, q].wait_recv()
                got[h, p, 2, part] = send(image_rows(h, p, q, part), image_rows(h, p, 2, part), along(h, 2, d))

    def last_arrive(p, q):
        for h in (0, 1):
            for part in (0, 1):
                got[h, p, q, part].wait_recv()

    for h in (0, 1):
        got[h, 1, 0] = send(image_rows(h, 0, 0), image_rows(h, 1, 0), along(h, 1, -1))
        got[h, 3, 0] = send(image_rows(h, 0, 0), image_rows(h, 3, 0), along(h, 1, 1))
    for h in (0, 1):
        text_forward(0, h)
    for h in (0, 1):
        to_second_axis(h, 0)

    first_axis_arrive(1)
    first_axis_arrive(3)
    text_arrive(1, 7, half=0)
    second_axis_arrive(0)
    text_arrive(1, 7, half=1)
    last_arrive(2, 0)
    for h in (0, 1):
        to_second_axis(h, 2)
    text_arrive(2, 6, half=0)
    second_axis_arrive(1)
    text_arrive(2, 6, half=1)
    second_axis_arrive(3)
    text_arrive(3, 5, half=0)
    second_axis_arrive(2)
    last_arrive(0, 2)
    text_arrive(3, 5, half=1)
    last_arrive(1, 2)
    last_arrive(3, 2)
    text_arrive(4, half=0)
    text_arrive(4, half=1)
    last_arrive(2, 2)
    for k in range(NZ):
        for h in (0, 1):
            got["s", k, h].wait_recv()

    teach_scale = tscale_ref[0, 0] * LOG2E
    learn_scale = sscale_ref[0, 0] * LOG2E
    grad_scale = sscale_ref[0, 0]
    lane = lax.broadcasted_iota(jnp.int32, (128, 128), 1)
    line = lax.broadcasted_iota(jnp.int32, (128, 128), 0)
    spot = line % 32 + 32 * (line // 64)
    learn_spot = lane == spot
    teach_spot = lane == spot + 64

    def unit(g, tg):
        r = pl.multiple_of(g * 128, 128)
        c = pl.multiple_of(tg * 256, 256)
        lses = []
        for ref, lo, hi, scale in ((learn, 0, ds, learn_scale), (teach, ds, img.shape[1], teach_scale)):
            logits = nt_dot(img[pl.ds(r, 128), lo:hi], txt[pl.ds(c, 256), lo:hi]) * scale
            ref[pl.ds(r, 128), pl.ds(c, 256)] = logits
            top = jnp.max(logits, axis=1, keepdims=True)
            row_l = top + jnp.log(jnp.sum(jnp.exp2(logits - top), axis=1, keepdims=True)) * LOG2E
            top = jnp.max(logits, axis=0, keepdims=True)
            col_l = top + jnp.log(jnp.sum(jnp.exp2(logits - top), axis=0, keepdims=True)) * LOG2E
            lses.append((row_l, col_l))
        packed = jnp.where(learn_spot, lses[0][0], 0.0) + jnp.where(teach_spot, lses[1][0], 0.0)
        row_part[tg, g] = jnp.sum(packed.reshape(4, 32, 128), axis=1)
        col_part[g, 0:1, pl.ds(c, 256)] = lses[0][1]
        col_part[g, 1:2, pl.ds(c, 256)] = lses[1][1]

    @pl.loop(0, 4)
    def _(tg):
        @pl.loop(0, 8)
        def _(g):
            unit(g, tg)

    low = lax.broadcasted_iota(jnp.int32, (1, 128), 1) < 64
    half0 = lax.broadcasted_iota(jnp.int32, (1, 128), 1) % 64 < 32
    row_local = join_lse([row_part[tg] for tg in range(4)])

    def block_row(dy, dx):
        return ((y + dy) % NY) * NX + (x + dx) % NX

    where_is = {key: (g, k) for g, keys in enumerate(HALF_BLOCKS) for k, key in enumerate(keys)}
    for dy in range(NY):
        for dx in range(NX):
            g0, k0 = where_is[0, dx, dy]
            g1, k1 = where_is[1, dy, dx]
            line0, line1 = row_local[g0, k0 : k0 + 1, :], row_local[g1, k1 : k1 + 1, :]
            row_stat[0, pl.ds(block_row(dy, dx), 1), :] = jnp.where(half0, line0, line1)
    row_got = [send(row_stat.at[0], row_in.at[d - 1], device(dx=d)) for d in (1, 2, 3)]

    col_local = join_lse([col_part[g] for g in range(8)])

    def text_place(k, sib):
        return (1 - core if sib else core) * NZ + (z + k) % NZ

    for tg, (k0, k1) in enumerate(TEXT_GROUPS):
        for sib in (0, 1):
            c = tg * 256 + sib * 128
            ls, lt = col_local[0:1, c : c + 128], col_local[1:2, c : c + 128]
            col_stat[0, pl.ds(text_place(k0, sib), 1), :] = jnp.where(low, ls, pltpu.roll(lt, 64, 1))
            col_stat[0, pl.ds(text_place(k1, sib), 1), :] = jnp.where(low, pltpu.roll(ls, 64, 1), lt)
    col_got = send(col_stat.at[0], col_in.at[0], device(sibling=True))

    for copy in row_got:
        copy.wait_recv()
    row_stat[1] = join_lse([row_stat[0]] + [row_in[i] for i in range(3)])
    row_got = [send(row_stat.at[1], row_in.at[2 + d], device(dy=d)) for d in (1, 2, 3)]
    col_got.wait_recv()
    col_stat[1] = join_lse([col_stat[0], col_in[0]])
    col_got = [send(col_stat.at[1], col_in.at[d], device(dz=d)) for d in range(1, NZ)]
    for copy in row_got:
        copy.wait_recv()
    row_stat[2] = join_lse([row_stat[1]] + [row_in[3 + i] for i in range(3)]) + 1.0
    for dy in range(NY):
        for dx in range(NX):
            whole = row_stat[2, pl.ds(block_row(dy, dx), 1), :]
            g0, k0 = where_is[0, dx, dy]
            g1, k1 = where_is[1, dy, dx]
            row_lse[g0, k0 : k0 + 1, :] = whole
            row_lse[g1, k1 : k1 + 1, :] = whole
    for copy in col_got:
        copy.wait_recv()
    col_stat[2] = join_lse([col_stat[1]] + [col_in[d] for d in range(1, NZ)]) + 1.0
    for tg, (k0, k1) in enumerate(TEXT_GROUPS):
        for sib in (0, 1):
            c = tg * 256 + sib * 128
            line0 = col_stat[2, pl.ds(text_place(k0, sib), 1), :]
            line1 = col_stat[2, pl.ds(text_place(k1, sib), 1), :]
            col_lse[0:1, c : c + 128] = jnp.where(low, line0, pltpu.roll(line1, 64, 1))
            col_lse[1:2, c : c + 128] = jnp.where(low, pltpu.roll(line0, 64, 1), line1)

    @pl.loop(0, 8)
    def _(g):
        r = pl.multiple_of(g * 128, 128)
        lines = jnp.broadcast_to(row_lse[g][:, None, :], (4, 32, 128)).reshape(128, 128)
        learn_row = jnp.sum(jnp.where(learn_spot, lines, 0.0), axis=1, keepdims=True)
        teach_row = jnp.sum(jnp.where(teach_spot, lines, 0.0), axis=1, keepdims=True)
        for tg in range(4):
            c = slice(tg * 256, tg * 256 + 256)
            s, t = learn[pl.ds(r, 128), c], teach[pl.ds(r, 128), c]
            value = (jnp.exp2(s - learn_row) - jnp.exp2(t - teach_row)) + (
                jnp.exp2(s - col_lse[0:1, c]) - jnp.exp2(t - col_lse[1:2, c])
            )
            weight[pl.ds(r, 128), c] = value.astype(BF16)

    text_got = []
    for tg in range(4):
        c = tg * 256 + 128
        part = tn_dot(weight[:, c : c + 128], img[:, :ds]) * grad_scale
        text_send[tg] = part.astype(BF16)
        text_got.append(send(text_send.at[tg], text_in.at[tg], device(sibling=True)))
    for g, keys in enumerate(HALF_BLOCKS):
        part = jnp.dot(weight[g * 128 : g * 128 + 128, :], txt[:, :ds], preferred_element_type=F32) * grad_scale
        for k, (h, p, q) in enumerate(keys):
            piece = part[k * 32 : k * 32 + 32, :]
            if q == 0:
                image_own[h, p * 32 : p * 32 + 32, :] = piece
            else:
                image_send[h, q - 1, p * 32 : p * 32 + 32, :] = piece.astype(BF16)
    image_got = [
        [send(image_send.at[h, q - 1], image_in.at[h, q - 1], along(h, 2, q)) for q in (1, 2, 3)] for h in (0, 1)
    ]
    for tg in range(4):
        c = tg * 256
        text_own[tg] = tn_dot(weight[:, c : c + 128], img[:, :ds]) * grad_scale
    for tg in range(4):
        text_got[tg].wait_recv()
        text_own[tg] = text_own[tg] + text_in[tg].astype(F32)
    text_send2[0] = text_own[0].astype(BF16)
    text_send2[1] = text_own[2].astype(BF16)
    text_half[...] = text_own[3, 64:128, :].astype(BF16)
    merge = [
        send(text_send2.at[1, pl.ds(0, 64)], text_in2.at[1, pl.ds(0, 64)], device(dz=1)),
        send(text_half.at[pl.ds(0, 32)], text_in2.at[2, pl.ds(0, 32)], device(dz=2)),
        send(text_send2.at[1, pl.ds(64, 64)], text_in2.at[1, pl.ds(64, 64)], device(dz=-1)),
        send(text_half.at[pl.ds(32, 32)], text_in2.at[2, pl.ds(32, 32)], device(dz=-2)),
    ]
    final = [
        send(text_send2.at[0, pl.ds(0, 64)], text_in2.at[0, pl.ds(0, 64)], device(dz=1)),
        send(text_send2.at[0, pl.ds(64, 64)], text_in2.at[0, pl.ds(64, 64)], device(dz=-1)),
    ]
    for h in (0, 1):
        for copy in image_got[h]:
            copy.wait_recv()
        image_sum[h] = image_own[h] + functools.reduce(jnp.add, [image_in[h, i].astype(F32) for i in range(3)])
        image_send2[h] = image_sum[h, 32:128, :].astype(BF16)
    image_got = []
    for h in (0, 1):
        for p in (1, 2, 3):
            at = pl.ds((p - 1) * 32, 32)
            image_got.append(send(image_send2.at[h, at], image_in2.at[h, at], along(h, 1, p)))
    for copy in merge:
        copy.wait_recv()
    joined = text_own[1] + text_in2[1].astype(F32)
    extra = text_in2[2, 0:64, :].astype(F32)
    text_in3[0, 0:32, :] = (joined[0:32] + extra[0:32]).astype(BF16)
    text_in3[0, 32:96, :] = joined[32:96].astype(BF16)
    text_in3[0, 96:128, :] = (joined[96:128] + extra[32:64]).astype(BF16)
    final += [
        send(text_in3.at[0, pl.ds(0, 64)], text_in3.at[1, pl.ds(0, 64)], device(dz=2)),
        send(text_in3.at[0, pl.ds(64, 64)], text_in3.at[1, pl.ds(64, 64)], device(dz=-2)),
    ]
    for copy in image_got:
        copy.wait_recv()
    for h in (0, 1):
        at = slice(h * 32, h * 32 + 32)
        total = image_sum[h, 0:32, :] + functools.reduce(
            jnp.add, [image_in2[h, i * 32 : i * 32 + 32, :].astype(F32) for i in range(3)]
        )
        image_out[at, :] = back_norm(total, si_ref[at, :])
    for copy in final:
        copy.wait_recv()
    total = text_own[3, 0:64, :]
    for ref, i in ((text_in2, 0), (text_in3, 1)):
        total = total + ref[i, 0:64, :].astype(F32) + ref[i, 64:128, :].astype(F32)
    text_out[...] = back_norm(total, st_ref[...])
    for copy in copies:
        copy.wait_send()


def body(student_image, student_text, teacher_image, teacher_text, teacher_scale, student_scale):
    own, ds = student_image.shape
    width = ds + teacher_image.shape[1]
    vmem = pl.BlockSpec(memory_space=pltpu.VMEM)
    smem = pl.BlockSpec(memory_space=pltpu.SMEM)
    out = jax.ShapeDtypeStruct((own, ds), F32)
    return pl.pallas_call(
        kernel,
        out_shape=(out, out),
        in_specs=[smem, smem, vmem, vmem, vmem, vmem],
        out_specs=(vmem, vmem),
        scratch_shapes=[
            pltpu.VMEM((1024, width), BF16),
            pltpu.VMEM((1024, width), BF16),
            pltpu.VMEM((1024, 1024), F32),
            pltpu.VMEM((1024, 1024), F32),
            pltpu.VMEM((1024, 1024), BF16),
            pltpu.VMEM((4, 8, 4, 128), F32),
            pltpu.VMEM((8, 2, 1024), F32),
            pltpu.VMEM((3, 16, 128), F32),
            pltpu.VMEM((3, 16, 128), F32),
            pltpu.VMEM((6, 16, 128), F32),
            pltpu.VMEM((8, 16, 128), F32),
            pltpu.VMEM((8, 4, 128), F32),
            pltpu.VMEM((2, 1024), F32),
            pltpu.VMEM((2, 128, ds), F32),
            pltpu.VMEM((2, 3, 128, ds), BF16),
            pltpu.VMEM((2, 3, 128, ds), BF16),
            pltpu.VMEM((2, 128, ds), F32),
            pltpu.VMEM((2, 96, ds), BF16),
            pltpu.VMEM((2, 96, ds), BF16),
            pltpu.VMEM((4, 128, ds), F32),
            pltpu.VMEM((4, 128, ds), BF16),
            pltpu.VMEM((4, 128, ds), BF16),
            pltpu.VMEM((2, 128, ds), BF16),
            pltpu.VMEM((3, 128, ds), BF16),
            pltpu.VMEM((64, ds), BF16),
            pltpu.VMEM((2, 128, ds), BF16),
            pltpu.SemaphoreType.DMA((COPIES,)),
            pltpu.SemaphoreType.DMA((COPIES,)),
        ],
        compiler_params=pltpu.CompilerParams(
            collective_id=0, has_side_effects=True, vmem_limit_bytes=48 * 1024 * 1024
        ),
    )(
        teacher_scale.reshape(1, 1), student_scale.reshape(1, 1),
        student_image, student_text, teacher_image, teacher_text,
    )


def solution(mesh):
    placed = P(("row", "col"), None)
    return jax.shard_map(
        body,
        mesh=mesh,
        in_specs=(placed, placed, placed, placed, P(), P()),
        out_specs=(placed, placed),
        check_vma=False,
    )
```

```python
import functools
import math

import jax
import jax.numpy as jnp
from jax import lax
from jax.experimental import pallas as pl
from jax.experimental.pallas import tpu as pltpu
from jax.sharding import PartitionSpec as P

EPSILON = 1e-12
MESH = pl.DeviceIdType.MESH
NX, NY, NZ = 4, 4, 8
LOG2E = math.log2(math.e)
F32, BF16 = jnp.float32, jnp.bfloat16
COPIES = 160

PAIRS = (
    ((0, 0), (1, 0)),
    ((3, 0), (0, 1)),
    ((0, 3), (2, 0)),
    ((1, 1), (1, 3)),
    ((3, 1), (3, 3)),
    ((2, 1), (2, 3)),
    ((0, 2), (1, 2)),
    ((3, 2), (2, 2)),
)
HALF_BLOCKS = tuple(tuple((h, p, q) for h in (0, 1) for p, q in pair) for pair in PAIRS)
IMAGE_ROW = {key: g * 128 + k * 32 for g, keys in enumerate(HALF_BLOCKS) for k, key in enumerate(keys)}
TEXT_BLOCKS = (
    (0, 0), (0, 1), (1, 0), (7, 0), (1, 1), (7, 1),
    (2, 0), (6, 0), (2, 1), (6, 1),
    (3, 0), (5, 0), (3, 1), (5, 1),
    (4, 0), (4, 1),
)
TEXT_ROW = {key: i * 64 for i, key in enumerate(TEXT_BLOCKS)}
COLUMNS = ((0, 384), (384, 640), (640, 896), (896, 1024))


def unit_rows(raw):
    values = raw.astype(F32)
    inverse = lax.rsqrt(jnp.sum(values * values, axis=-1, keepdims=True) + EPSILON)
    return values * inverse, inverse


def join_lse(parts):
    top = functools.reduce(jnp.maximum, parts)
    total = functools.reduce(jnp.add, [jnp.exp2(part - top) for part in parts])
    return top + jnp.log(total) * LOG2E


def back_norm(grad, raw):
    unit, inverse = unit_rows(raw)
    return inverse * (grad - unit * jnp.sum(unit * grad, axis=-1, keepdims=True))


def nt_dot(a, b):
    return lax.dot_general(a, b, (((1,), (1,)), ((), ())), preferred_element_type=F32)


def tn_dot(a, b):
    return lax.dot_general(a, b, (((0,), (0,)), ((), ())), preferred_element_type=F32)


def kernel(
    tscale_ref, sscale_ref, si_hbm, st_hbm, ti_hbm, tt_hbm, image_out, text_out,
    si_ref, st_ref, ti_ref, tt_ref, img, txt, teach, learn, weight, row_part, col_part, row_stat, col_stat, row_in, col_in, row_lse, col_lse,
    image_own, image_send, image_in, image_sum, image_send2, image_in2,
    text_own, text_send, text_in, text_send2, text_in2, text_send3, text_in3,
    send_sem, recv_sem, load_sem,
):
    ds = si_ref.shape[1]
    row, col = lax.axis_index("row"), lax.axis_index("col")
    y, core = row // 2, row % 2
    z, x = col // NX, col % NX

    def device(dx=0, dy=0, dz=0, sibling=False):
        c = 1 - core if sibling else core
        return (((y + dy) % NY) * 2 + c, ((z + dz) % NZ) * NX + (x + dx) % NX)

    def along(half, axis, d):
        return device(dx=d) if (half == 0) == (axis == 1) else device(dy=d)

    copies = []

    def send(src, dst, target):
        i = len(copies)
        copy = pltpu.make_async_remote_copy(
            src_ref=src, dst_ref=dst, send_sem=send_sem.at[i], recv_sem=recv_sem.at[i],
            device_id=target, device_id_type=MESH,
        )
        copy.start()
        copies.append(copy)
        return copy

    barrier = pltpu.get_barrier_semaphore()
    peers = [device(dx=1), device(dx=-1), device(dy=1), device(dy=-1), device(dz=1), device(dz=-1)]
    peers += [device(sibling=True)]
    for peer in peers:
        pl.semaphore_signal(barrier, inc=1, device_id=peer, device_id_type=MESH)

    loads = [
        pltpu.make_async_copy(src, dst, load_sem.at[i])
        for i, (src, dst) in enumerate(((ti_hbm, ti_ref), (tt_hbm, tt_ref), (si_hbm, si_ref), (st_hbm, st_ref)))
    ]
    for load in loads:
        load.start()
    for load in loads:
        load.wait()

    own_text = TEXT_ROW[(0, 0)]
    for start, size in ((0, 32), (32, 32)):
        for h_ref, lo, hi in ((si_ref, 0, ds), (ti_ref, ds, img.shape[1])):
            at = IMAGE_ROW[(start // 32, 0, 0)]
            img[at : at + size, lo:hi] = unit_rows(h_ref[start : start + size, :])[0].astype(BF16)
    for h_ref, lo, hi in ((st_ref, 0, ds), (tt_ref, ds, img.shape[1])):
        txt[own_text : own_text + 64, lo:hi] = unit_rows(h_ref[...])[0].astype(BF16)

    pl.semaphore_wait(barrier, len(peers))

    got = {}

    def rows(ref, at, size):
        return ref.at[pl.ds(at, size), :]

    def text_rows(k, part, size=16, sib=0):
        return rows(txt, TEXT_ROW[(k, sib)] + part * size, size)

    def image_rows(h, p, q, part=None):
        at = IMAGE_ROW[(h, p, q)]
        return rows(img, at, 32) if part is None else rows(img, at + part * 16, 16)

    def to_second_axis(h, p):
        got[h, p, 1] = send(image_rows(h, p, 0), image_rows(h, p, 1), along(h, 2, -1))
        got[h, p, 3] = send(image_rows(h, p, 0), image_rows(h, p, 3), along(h, 2, 1))

    def text_send_on(k, j, part, d):
        got["t", j, part] = send(text_rows(k, part), text_rows(j, part), device(dz=d))

    def text_to_sibling(k, half):
        got["s", k, half] = send(text_rows(k, half, 32), text_rows(k, half, 32, 1), device(sibling=True))

    def text_arrive(k, step):
        for slot, part, d in ((k, step, -1), (NZ - k, 3 - step, 1)):
            got["t", slot, part].wait_recv()
            if k < 3 or step < 2:
                text_send_on(slot, slot - d if k < 3 else 4, part, d)
            if step % 2:
                text_to_sibling(slot, part // 2)

    def text_arrive_last(step):
        for part in (step, 3 - step):
            got["t", 4, part].wait_recv()
            if step % 2:
                text_to_sibling(4, part // 2)

    def sibling_arrive(*ks):
        for k in ks:
            for half in (0, 1):
                got["s", k, half].wait_recv()

    def first_axis_arrive():
        for h in (0, 1):
            for p, part, d in ((1, 0, -1), (3, 1, 1)):
                got[h, p, 0].wait_recv()
                got[h, 2, 0, part] = send(image_rows(h, p, 0, part), image_rows(h, 2, 0, part), along(h, 1, d))
        for p in (1, 3):
            for h in (0, 1):
                to_second_axis(h, p)

    def second_axis_arrive(p):
        for h in (0, 1):
            for q, part, d in ((1, 0, -1), (3, 1, 1)):
                got[h, p, q].wait_recv()
                got[h, p, 2, part] = send(image_rows(h, p, q, part), image_rows(h, p, 2, part), along(h, 2, d))

    def last_arrive(p, q):
        for h in (0, 1):
            for part in (0, 1):
                got[h, p, q, part].wait_recv()

    teach_scale = tscale_ref[0, 0] * LOG2E
    learn_scale = sscale_ref[0, 0] * LOG2E
    grad_scale = sscale_ref[0, 0]
    lane = lax.broadcasted_iota(jnp.int32, (128, 128), 1)
    line = lax.broadcasted_iota(jnp.int32, (128, 128), 0)
    spot = line % 32 + 32 * (line // 64)
    learn_spot = lane == spot
    teach_spot = lane == spot + 64

    def logits(first, last, *blocks):
        r = slice(first * 128, last * 128)
        for b in blocks:
            c = slice(*COLUMNS[b])
            for ref, lo, hi, scale in ((learn, 0, ds, learn_scale), (teach, ds, img.shape[1], teach_scale)):
                ref[r, c] = nt_dot(img[r, lo:hi], txt[c, lo:hi]) * scale

        @pl.loop(first, last)
        def _(g):
            r = pl.multiple_of(g * 128, 128)
            for b in blocks:
                c = slice(*COLUMNS[b])
                row_ls = []
                for i, ref in enumerate((learn, teach)):
                    block = ref[pl.ds(r, 128), c]
                    top = jnp.max(block, axis=1, keepdims=True)
                    total = jnp.sum(jnp.exp2(block - top), axis=1, keepdims=True)
                    row_ls.append(top + jnp.log(total) * LOG2E)
                    top = jnp.max(block, axis=0, keepdims=True)
                    total = jnp.sum(jnp.exp2(block - top), axis=0, keepdims=True)
                    col_part[g, i : i + 1, c] = top + jnp.log(total) * LOG2E
                packed = jnp.where(learn_spot, row_ls[0], 0.0) + jnp.where(teach_spot, row_ls[1], 0.0)
                row_part[b, g] = jnp.sum(packed.reshape(4, 32, 128), axis=1)

    for step in range(4):
        text_send_on(0, 1, step, -1)
        text_send_on(0, 7, 3 - step, 1)
        if step == 0:
            for h in (0, 1):
                got[h, 1, 0] = send(image_rows(h, 0, 0), image_rows(h, 1, 0), along(h, 1, -1))
                got[h, 3, 0] = send(image_rows(h, 0, 0), image_rows(h, 3, 0), along(h, 1, 1))
    for h in (0, 1):
        to_second_axis(h, 0)
    for half in (0, 1):
        text_to_sibling(0, half)

    text_arrive(1, 0)
    first_axis_arrive()
    text_arrive(1, 1)
    text_arrive(1, 2)
    text_arrive(1, 3)
    second_axis_arrive(0)
    last_arrive(2, 0)
    for h in (0, 1):
        to_second_axis(h, 2)
    text_arrive(2, 0)
    sibling_arrive(0, 1, 7)
    logits(0, 3, 0)
    text_arrive(2, 1)
    second_axis_arrive(1)
    text_arrive(2, 2)
    logits(3, 4, 0)
    text_arrive(2, 3)
    second_axis_arrive(3)
    text_arrive(3, 0)
    logits(4, 5, 0)
    sibling_arrive(2, 6)
    logits(0, 3, 1)
    text_arrive(3, 1)
    logits(3, 5, 1)
    text_arrive(3, 2)
    second_axis_arrive(2)
    text_arrive(3, 3)
    logits(5, 6, 0, 1)
    text_arrive_last(0)
    last_arrive(0, 2)
    last_arrive(1, 2)
    sibling_arrive(3, 5)
    logits(6, 7, 0, 1)
    logits(0, 4, 2)
    text_arrive_last(1)
    logits(4, 7, 2)
    last_arrive(3, 2)
    last_arrive(2, 2)
    logits(7, 8, 0, 1, 2)
    sibling_arrive(4)
    logits(0, 8, 3)

    low = lax.broadcasted_iota(jnp.int32, (1, 128), 1) < 64
    half0 = lax.broadcasted_iota(jnp.int32, (1, 128), 1) % 64 < 32
    row_local = join_lse([row_part[tg] for tg in range(4)])

    def block_row(dy, dx):
        return ((y + dy) % NY) * NX + (x + dx) % NX

    where_is = {key: (g, k) for g, keys in enumerate(HALF_BLOCKS) for k, key in enumerate(keys)}
    for dy in range(NY):
        for dx in range(NX):
            g0, k0 = where_is[0, dx, dy]
            g1, k1 = where_is[1, dy, dx]
            line0, line1 = row_local[g0, k0 : k0 + 1, :], row_local[g1, k1 : k1 + 1, :]
            row_stat[0, pl.ds(block_row(dy, dx), 1), :] = jnp.where(half0, line0, line1)
    row_got = [send(row_stat.at[0], row_in.at[d - 1], device(dx=d)) for d in (1, 2, 3)]

    col_local = join_lse([col_part[g] for g in range(8)])

    def text_place(k, sib):
        return (1 - core if sib else core) * NZ + (z + k) % NZ

    for tile in range(8):
        c = slice(tile * 128, tile * 128 + 128)
        ls, lt = col_local[0:1, c], col_local[1:2, c]
        first, second = TEXT_BLOCKS[2 * tile : 2 * tile + 2]
        col_stat[0, pl.ds(text_place(*first), 1), :] = jnp.where(low, ls, pltpu.roll(lt, 64, 1))
        col_stat[0, pl.ds(text_place(*second), 1), :] = jnp.where(low, pltpu.roll(ls, 64, 1), lt)
    col_got = send(col_stat.at[0], col_in.at[0], device(sibling=True))

    for copy in row_got:
        copy.wait_recv()
    row_stat[1] = join_lse([row_stat[0]] + [row_in[i] for i in range(3)])
    row_got = [send(row_stat.at[1], row_in.at[2 + d], device(dy=d)) for d in (1, 2, 3)]
    col_got.wait_recv()
    col_stat[1] = join_lse([col_stat[0], col_in[0]])
    col_got = [send(col_stat.at[1], col_in.at[d], device(dz=d)) for d in range(1, NZ)]
    for copy in row_got:
        copy.wait_recv()
    row_stat[2] = join_lse([row_stat[1]] + [row_in[3 + i] for i in range(3)]) + 1.0
    for dy in range(NY):
        for dx in range(NX):
            whole = row_stat[2, pl.ds(block_row(dy, dx), 1), :]
            g0, k0 = where_is[0, dx, dy]
            g1, k1 = where_is[1, dy, dx]
            row_lse[g0, k0 : k0 + 1, :] = whole
            row_lse[g1, k1 : k1 + 1, :] = whole
    for copy in col_got:
        copy.wait_recv()
    col_stat[2] = join_lse([col_stat[1]] + [col_in[d] for d in range(1, NZ)]) + 1.0
    for tile in range(8):
        c = slice(tile * 128, tile * 128 + 128)
        first, second = TEXT_BLOCKS[2 * tile : 2 * tile + 2]
        line0 = col_stat[2, pl.ds(text_place(*first), 1), :]
        line1 = col_stat[2, pl.ds(text_place(*second), 1), :]
        col_lse[0:1, c] = jnp.where(low, line0, pltpu.roll(line1, 64, 1))
        col_lse[1:2, c] = jnp.where(low, pltpu.roll(line0, 64, 1), line1)

    @pl.loop(0, 8)
    def _(g):
        r = pl.multiple_of(g * 128, 128)
        lines = jnp.broadcast_to(row_lse[g][:, None, :], (4, 32, 128)).reshape(128, 128)
        learn_row = jnp.sum(jnp.where(learn_spot, lines, 0.0), axis=1, keepdims=True)
        teach_row = jnp.sum(jnp.where(teach_spot, lines, 0.0), axis=1, keepdims=True)
        for tg in range(4):
            c = slice(tg * 256, tg * 256 + 256)
            s, t = learn[pl.ds(r, 128), c], teach[pl.ds(r, 128), c]
            value = (jnp.exp2(s - learn_row) - jnp.exp2(t - teach_row)) + (
                jnp.exp2(s - col_lse[0:1, c]) - jnp.exp2(t - col_lse[1:2, c])
            )
            weight[pl.ds(r, 128), c] = value.astype(BF16)

    text_got = []

    def text_grads(*tiles):
        for tile in tiles:
            c = slice(tile * 128, tile * 128 + 128)
            part = tn_dot(weight[:, c], img[:, :ds]) * grad_scale
            for i, (k, sib) in enumerate(TEXT_BLOCKS[2 * tile : 2 * tile + 2]):
                piece = part[i * 64 : i * 64 + 64, :]
                if sib:
                    text_send[k] = piece.astype(BF16)
                    text_got.append(send(text_send.at[k], text_in.at[k], device(sibling=True)))
                else:
                    text_own[k] = piece

    text_grads(0, 2, 4, 6, 7)
    for g, keys in enumerate(HALF_BLOCKS):
        part = jnp.dot(weight[g * 128 : g * 128 + 128, :], txt[:, :ds], preferred_element_type=F32) * grad_scale
        for k, (h, p, q) in enumerate(keys):
            piece = part[k * 32 : k * 32 + 32, :]
            if q == 0:
                image_own[h, p * 32 : p * 32 + 32, :] = piece
            else:
                image_send[h, q - 1, p * 32 : p * 32 + 32, :] = piece.astype(BF16)
    image_got = [
        [send(image_send.at[h, q - 1], image_in.at[h, q - 1], along(h, 2, q)) for q in (1, 2, 3)] for h in (0, 1)
    ]
    text_grads(1, 3, 5)
    for copy in text_got:
        copy.wait_recv()
    for k in range(NZ):
        text_own[k] = text_own[k] + text_in[k].astype(F32)
    for i, k in enumerate((1, 7, 3, 5, 4)):
        text_send2[i] = text_own[k].astype(BF16)
    merge = [
        send(text_send2.at[2], text_in2.at[2], device(dz=1)),
        send(text_send2.at[4, pl.ds(0, 32)], text_in2.at[4, pl.ds(0, 32)], device(dz=2)),
        send(text_send2.at[3], text_in2.at[3], device(dz=-1)),
        send(text_send2.at[4, pl.ds(32, 32)], text_in2.at[4, pl.ds(32, 32)], device(dz=-2)),
    ]
    final = [
        send(text_send2.at[0], text_in2.at[0], device(dz=1)),
        send(text_send2.at[1], text_in2.at[1], device(dz=-1)),
    ]
    for h in (0, 1):
        for copy in image_got[h]:
            copy.wait_recv()
        image_sum[h] = image_own[h] + functools.reduce(jnp.add, [image_in[h, i].astype(F32) for i in range(3)])
        image_send2[h] = image_sum[h, 32:128, :].astype(BF16)
    image_got = []
    for h in (0, 1):
        for p in (1, 2, 3):
            at = pl.ds((p - 1) * 32, 32)
            image_got.append(send(image_send2.at[h, at], image_in2.at[h, at], along(h, 1, p)))
    for copy in merge:
        copy.wait_recv()
    for i, k, h in ((0, 2, 0), (1, 6, 1)):
        joined = text_own[k] + text_in2[2 + i].astype(F32)
        near = slice(h * 32, h * 32 + 32)
        far = slice(32 - h * 32, 64 - h * 32)
        text_send3[i, near, :] = (joined[near] + text_in2[4, near, :].astype(F32)).astype(BF16)
        text_send3[i, far, :] = joined[far].astype(BF16)
        final.append(send(text_send3.at[i], text_in3.at[i], device(dz=2 - 4 * i)))
    for copy in image_got:
        copy.wait_recv()
    for h in (0, 1):
        at = slice(h * 32, h * 32 + 32)
        total = image_sum[h, 0:32, :] + functools.reduce(
            jnp.add, [image_in2[h, i * 32 : i * 32 + 32, :].astype(F32) for i in range(3)]
        )
        image_out[at, :] = back_norm(total, si_ref[at, :])
    for copy in final:
        copy.wait_recv()
    total = text_own[0]
    for ref in (text_in2, text_in3):
        total = total + ref[0].astype(F32) + ref[1].astype(F32)
    text_out[...] = back_norm(total, st_ref[...])
    for copy in copies:
        copy.wait_send()


def body(student_image, student_text, teacher_image, teacher_text, teacher_scale, student_scale):
    own, ds = student_image.shape
    width = ds + teacher_image.shape[1]
    vmem = pl.BlockSpec(memory_space=pltpu.VMEM)
    smem = pl.BlockSpec(memory_space=pltpu.SMEM)
    hbm = pl.BlockSpec(memory_space=pltpu.HBM)
    out = jax.ShapeDtypeStruct((own, ds), F32)
    return pl.pallas_call(
        kernel,
        out_shape=(out, out),
        in_specs=[smem, smem, hbm, hbm, hbm, hbm],
        out_specs=(vmem, vmem),
        scratch_shapes=[
            pltpu.VMEM((own, ds), BF16),
            pltpu.VMEM((own, ds), BF16),
            pltpu.VMEM((own, width - ds), BF16),
            pltpu.VMEM((own, width - ds), BF16),
            pltpu.VMEM((1024, width), BF16),
            pltpu.VMEM((1024, width), BF16),
            pltpu.VMEM((1024, 1024), F32),
            pltpu.VMEM((1024, 1024), F32),
            pltpu.VMEM((1024, 1024), BF16),
            pltpu.VMEM((4, 8, 4, 128), F32),
            pltpu.VMEM((8, 2, 1024), F32),
            pltpu.VMEM((3, 16, 128), F32),
            pltpu.VMEM((3, 16, 128), F32),
            pltpu.VMEM((6, 16, 128), F32),
            pltpu.VMEM((8, 16, 128), F32),
            pltpu.VMEM((8, 4, 128), F32),
            pltpu.VMEM((2, 1024), F32),
            pltpu.VMEM((2, 128, ds), F32),
            pltpu.VMEM((2, 3, 128, ds), BF16),
            pltpu.VMEM((2, 3, 128, ds), BF16),
            pltpu.VMEM((2, 128, ds), F32),
            pltpu.VMEM((2, 96, ds), BF16),
            pltpu.VMEM((2, 96, ds), BF16),
            pltpu.VMEM((NZ, 64, ds), F32),
            pltpu.VMEM((NZ, 64, ds), BF16),
            pltpu.VMEM((NZ, 64, ds), BF16),
            pltpu.VMEM((5, 64, ds), BF16),
            pltpu.VMEM((5, 64, ds), BF16),
            pltpu.VMEM((2, 64, ds), BF16),
            pltpu.VMEM((2, 64, ds), BF16),
            pltpu.SemaphoreType.DMA((COPIES,)),
            pltpu.SemaphoreType.DMA((COPIES,)),
            pltpu.SemaphoreType.DMA((4,)),
        ],
        compiler_params=pltpu.CompilerParams(
            collective_id=0, has_side_effects=True, vmem_limit_bytes=48 * 1024 * 1024
        ),
    )(
        teacher_scale.reshape(1, 1), student_scale.reshape(1, 1),
        student_image, student_text, teacher_image, teacher_text,
    )


def solution(mesh):
    placed = P(("row", "col"), None)
    return jax.shard_map(
        body,
        mesh=mesh,
        in_specs=(placed, placed, placed, placed, P(), P()),
        out_specs=(placed, placed),
        check_vma=False,
    )
```

```python
import functools
import math

import jax
import jax.numpy as jnp
from jax import lax
from jax.experimental import pallas as pl
from jax.experimental.pallas import tpu as pltpu
from jax.sharding import PartitionSpec as P

EPSILON = 1e-12
MESH = pl.DeviceIdType.MESH
NX, NY, NZ = 4, 4, 8
LOG2E = math.log2(math.e)
F32, BF16 = jnp.float32, jnp.bfloat16
COPIES = 160

PAIRS = (
    ((0, 0), (1, 0)),
    ((3, 0), (0, 1)),
    ((0, 3), (2, 0)),
    ((1, 1), (1, 3)),
    ((3, 1), (3, 3)),
    ((2, 1), (2, 3)),
    ((0, 2), (1, 2)),
    ((3, 2), (2, 2)),
)
HALF_BLOCKS = tuple(tuple((h, p, q) for h in (0, 1) for p, q in pair) for pair in PAIRS)
IMAGE_ROW = {key: g * 128 + k * 32 for g, keys in enumerate(HALF_BLOCKS) for k, key in enumerate(keys)}
TEXT_BLOCKS = (
    (0, 0), (0, 1), (1, 0), (7, 0), (1, 1), (7, 1),
    (2, 0), (6, 0), (2, 1), (6, 1),
    (3, 0), (5, 0), (3, 1), (5, 1),
    (4, 0), (4, 1),
)
TEXT_ROW = {key: i * 64 for i, key in enumerate(TEXT_BLOCKS)}
COLUMNS = ((0, 384), (384, 640), (640, 896), (896, 1024))


def unit_rows(raw):
    values = raw.astype(F32)
    inverse = lax.rsqrt(jnp.sum(values * values, axis=-1, keepdims=True) + EPSILON)
    return values * inverse, inverse


def join_lse(parts):
    top = functools.reduce(jnp.maximum, parts)
    total = functools.reduce(jnp.add, [jnp.exp2(part - top) for part in parts])
    return top + jnp.log(total) * LOG2E


def back_norm(grad, raw):
    unit, inverse = unit_rows(raw)
    return inverse * (grad - unit * jnp.sum(unit * grad, axis=-1, keepdims=True))


def nt_dot(a, b):
    return lax.dot_general(a, b, (((1,), (1,)), ((), ())), preferred_element_type=F32)


def tn_dot(a, b):
    return lax.dot_general(a, b, (((0,), (0,)), ((), ())), preferred_element_type=F32)


def kernel(
    tscale_ref, sscale_ref, si_hbm, st_hbm, ti_hbm, tt_hbm, image_out, text_out,
    si_ref, st_ref, ti_ref, tt_ref, img, txt, teach, learn, weight, row_part, col_part, row_stat, col_stat, row_in, col_in,
    row_local, col_local, row_whole, row_scale, col_scale, by_row, by_col,
    image_own, image_send, image_in, image_sum, image_send2, image_in2,
    text_own, text_send, text_in, text_send2, text_in2, text_send3, text_in3,
    send_sem, recv_sem, load_sem,
):
    ds = si_ref.shape[1]
    row, col = lax.axis_index("row"), lax.axis_index("col")
    y, core = row // 2, row % 2
    z, x = col // NX, col % NX

    def device(dx=0, dy=0, dz=0, sibling=False):
        c = 1 - core if sibling else core
        return (((y + dy) % NY) * 2 + c, ((z + dz) % NZ) * NX + (x + dx) % NX)

    def along(half, axis, d):
        return device(dx=d) if (half == 0) == (axis == 1) else device(dy=d)

    copies = []

    def send(src, dst, target):
        i = len(copies)
        copy = pltpu.make_async_remote_copy(
            src_ref=src, dst_ref=dst, send_sem=send_sem.at[i], recv_sem=recv_sem.at[i],
            device_id=target, device_id_type=MESH,
        )
        copy.start()
        copies.append(copy)
        return copy

    barrier = pltpu.get_barrier_semaphore()
    peers = [device(dx=1), device(dx=-1), device(dy=1), device(dy=-1), device(dz=1), device(dz=-1)]
    peers += [device(sibling=True)]
    for peer in peers:
        pl.semaphore_signal(barrier, inc=1, device_id=peer, device_id_type=MESH)

    loads = [
        pltpu.make_async_copy(src, dst, load_sem.at[i])
        for i, (src, dst) in enumerate(((ti_hbm, ti_ref), (tt_hbm, tt_ref), (si_hbm, si_ref), (st_hbm, st_ref)))
    ]
    for load in loads:
        load.start()
    for load in loads:
        load.wait()

    own_text = TEXT_ROW[(0, 0)]
    for start, size in ((0, 32), (32, 32)):
        for h_ref, lo, hi in ((si_ref, 0, ds), (ti_ref, ds, img.shape[1])):
            at = IMAGE_ROW[(start // 32, 0, 0)]
            img[at : at + size, lo:hi] = unit_rows(h_ref[start : start + size, :])[0].astype(BF16)
    for h_ref, lo, hi in ((st_ref, 0, ds), (tt_ref, ds, img.shape[1])):
        txt[own_text : own_text + 64, lo:hi] = unit_rows(h_ref[...])[0].astype(BF16)

    pl.semaphore_wait(barrier, len(peers))

    got = {}

    def rows(ref, at, size):
        return ref.at[pl.ds(at, size), :]

    def text_rows(k, part, size=16, sib=0):
        return rows(txt, TEXT_ROW[(k, sib)] + part * size, size)

    def image_rows(h, p, q, part=None):
        at = IMAGE_ROW[(h, p, q)]
        return rows(img, at, 32) if part is None else rows(img, at + part * 16, 16)

    def to_second_axis(h, p):
        got[h, p, 1] = send(image_rows(h, p, 0), image_rows(h, p, 1), along(h, 2, -1))
        got[h, p, 3] = send(image_rows(h, p, 0), image_rows(h, p, 3), along(h, 2, 1))

    def text_send_on(k, j, part, d):
        got["t", j, part] = send(text_rows(k, part), text_rows(j, part), device(dz=d))

    def text_to_sibling(k, half):
        got["s", k, half] = send(text_rows(k, half, 32), text_rows(k, half, 32, 1), device(sibling=True))

    def text_arrive(k, step):
        for slot, part, d in ((k, step, -1), (NZ - k, 3 - step, 1)):
            got["t", slot, part].wait_recv()
            if k < 3 or step < 2:
                text_send_on(slot, slot - d if k < 3 else 4, part, d)
            if step % 2:
                text_to_sibling(slot, part // 2)

    def text_arrive_last(step):
        for part in (step, 3 - step):
            got["t", 4, part].wait_recv()
            if step % 2:
                text_to_sibling(4, part // 2)

    def sibling_arrive(*ks):
        for k in ks:
            for half in (0, 1):
                got["s", k, half].wait_recv()

    def first_axis_arrive():
        for h in (0, 1):
            for p, part, d in ((1, 0, -1), (3, 1, 1)):
                got[h, p, 0].wait_recv()
                got[h, 2, 0, part] = send(image_rows(h, p, 0, part), image_rows(h, 2, 0, part), along(h, 1, d))
        for p in (1, 3):
            for h in (0, 1):
                to_second_axis(h, p)

    def second_axis_arrive(p):
        for h in (0, 1):
            for q, part, d in ((1, 0, -1), (3, 1, 1)):
                got[h, p, q].wait_recv()
                got[h, p, 2, part] = send(image_rows(h, p, q, part), image_rows(h, p, 2, part), along(h, 2, d))

    def last_arrive(p, q):
        for h in (0, 1):
            for part in (0, 1):
                got[h, p, q, part].wait_recv()

    teach_scale = tscale_ref[0, 0] * LOG2E
    learn_scale = sscale_ref[0, 0] * LOG2E
    grad_scale = sscale_ref[0, 0]
    lane = lax.broadcasted_iota(jnp.int32, (128, 128), 1)
    line = lax.broadcasted_iota(jnp.int32, (128, 128), 0)
    spot = line % 32 + 32 * (line // 64)
    learn_spot = lane == spot
    teach_spot = lane == spot + 64

    def logits(first, last, *blocks):
        r = slice(first * 128, last * 128)
        for b in blocks:
            c = slice(*COLUMNS[b])
            for ref, lo, hi, scale in ((learn, 0, ds, learn_scale), (teach, ds, img.shape[1], teach_scale)):
                ref[r, c] = nt_dot(img[r, lo:hi], txt[c, lo:hi]) * scale

        for g in range(first, last):
            r = g * 128
            for b in blocks:
                c = slice(*COLUMNS[b])
                row_ls = []
                for i, ref in enumerate((learn, teach)):
                    block = ref[pl.ds(r, 128), c]
                    top = jnp.max(block, axis=1, keepdims=True)
                    total = jnp.sum(jnp.exp2(block - top), axis=1, keepdims=True)
                    row_ls.append(top + jnp.log(total) * LOG2E)
                    top = jnp.max(block, axis=0, keepdims=True)
                    total = jnp.sum(jnp.exp2(block - top), axis=0, keepdims=True)
                    col_part[g, i : i + 1, c] = top + jnp.log(total) * LOG2E
                packed = jnp.where(learn_spot, row_ls[0], 0.0) + jnp.where(teach_spot, row_ls[1], 0.0)
                row_part[b, g] = jnp.sum(packed.reshape(4, 32, 128), axis=1)

    for step in range(4):
        text_send_on(0, 1, step, -1)
        text_send_on(0, 7, 3 - step, 1)
        if step == 0:
            for h in (0, 1):
                got[h, 1, 0] = send(image_rows(h, 0, 0), image_rows(h, 1, 0), along(h, 1, -1))
                got[h, 3, 0] = send(image_rows(h, 0, 0), image_rows(h, 3, 0), along(h, 1, 1))
    for h in (0, 1):
        to_second_axis(h, 0)
    for half in (0, 1):
        text_to_sibling(0, half)

    text_arrive(1, 0)
    first_axis_arrive()
    text_arrive(1, 1)
    text_arrive(1, 2)
    text_arrive(1, 3)
    second_axis_arrive(0)
    last_arrive(2, 0)
    for h in (0, 1):
        to_second_axis(h, 2)
    text_arrive(2, 0)
    sibling_arrive(0, 1, 7)
    logits(0, 3, 0)
    text_arrive(2, 1)
    second_axis_arrive(1)
    text_arrive(2, 2)
    logits(3, 4, 0)
    text_arrive(2, 3)
    second_axis_arrive(3)
    text_arrive(3, 0)
    logits(4, 5, 0)
    sibling_arrive(2, 6)
    logits(0, 3, 1)
    text_arrive(3, 1)
    logits(3, 5, 1)
    text_arrive(3, 2)
    second_axis_arrive(2)
    text_arrive(3, 3)
    logits(5, 6, 0, 1)
    text_arrive_last(0)
    last_arrive(0, 2)
    last_arrive(1, 2)
    sibling_arrive(3, 5)
    logits(6, 7, 0, 1)
    logits(0, 4, 2)
    text_arrive_last(1)
    logits(4, 7, 2)
    last_arrive(3, 2)
    last_arrive(2, 2)
    logits(7, 8, 0, 1, 2)
    sibling_arrive(4)
    logits(0, 8, 3)

    low = lax.broadcasted_iota(jnp.int32, (1, 128), 1) < 64
    half0 = lax.broadcasted_iota(jnp.int32, (1, 128), 1) % 64 < 32
    where_is = {key: (g, k) for g, keys in enumerate(HALF_BLOCKS) for k, key in enumerate(keys)}
    row_places = [
        (((y + dy) % NY) * NX + (x + dx) % NX, where_is[0, dx, dy], where_is[1, dy, dx])
        for dy in range(NY)
        for dx in range(NX)
    ]
    col_places = [(1 - core if sib else core) * NZ + (z + k) % NZ for k, sib in TEXT_BLOCKS]

    def spread(lines):
        lines = jnp.broadcast_to(lines[:, None, :], (4, 32, 128)).reshape(128, 128)
        for mask in (learn_spot, teach_spot):
            yield jnp.broadcast_to(jnp.sum(jnp.where(mask, lines, 0.0), axis=1, keepdims=True), (128, 128))

    col_local[...] = join_lse([col_part[g] for g in range(8)])
    for tile in range(8):
        c = slice(tile * 128, tile * 128 + 128)
        ls, lt = col_local[0:1, c], col_local[1:2, c]
        first, second = col_places[2 * tile : 2 * tile + 2]
        col_stat[0, pl.ds(first, 1), :] = jnp.where(low, ls, pltpu.roll(lt, 64, 1))
        col_stat[0, pl.ds(second, 1), :] = jnp.where(low, pltpu.roll(ls, 64, 1), lt)
    col_got = send(col_stat.at[0], col_in.at[0], device(sibling=True))
    row_local[...] = join_lse([row_part[b] for b in range(len(COLUMNS))])
    for place, (g0, k0), (g1, k1) in row_places:
        row_stat[0, pl.ds(place, 1), :] = jnp.where(half0, row_local[g0, k0 : k0 + 1, :], row_local[g1, k1 : k1 + 1, :])
    row_got = [send(row_stat.at[0], row_in.at[d - 1], device(dx=d)) for d in (2, 1, 3)]

    def local_softmax(*groups):
        for g in groups:
            r = slice(g * 128, g * 128 + 128)
            row_ls = list(spread(row_local[g]))
            for tile in range(8):
                c = slice(tile * 128, tile * 128 + 128)
                for i, ref in enumerate((learn, teach)):
                    block = ref[r, c] - 1.0
                    by_row[i, r, c] = jnp.exp2(block - row_ls[i])
                    by_col[i, r, c] = jnp.exp2(block - col_local[i : i + 1, c])

    local_softmax(0, 1)
    col_got.wait_recv()
    col_stat[1] = join_lse([col_stat[0], col_in[0]])
    col_got = [send(col_stat.at[1], col_in.at[d], device(dz=d)) for d in (4, 3, 5, 2, 6, 1, 7)]
    local_softmax(2, 3, 4)
    for copy in row_got:
        copy.wait_recv()
    row_stat[1] = join_lse([row_stat[0]] + [row_in[i] for i in range(3)])
    row_got = [send(row_stat.at[1], row_in.at[2 + d], device(dy=d)) for d in (2, 1, 3)]
    local_softmax(5, 6, 7)
    for copy in col_got:
        copy.wait_recv()
    col_stat[2] = join_lse([col_stat[1]] + [col_in[d] for d in range(1, NZ)])
    for tile in range(8):
        c = slice(tile * 128, tile * 128 + 128)
        first, second = col_places[2 * tile : 2 * tile + 2]
        line0 = col_stat[2, pl.ds(first, 1), :]
        line1 = col_stat[2, pl.ds(second, 1), :]
        col_scale[0:1, c] = jnp.exp2(col_local[0:1, c] - jnp.where(low, line0, pltpu.roll(line1, 64, 1)))
        col_scale[1:2, c] = jnp.exp2(col_local[1:2, c] - jnp.where(low, pltpu.roll(line0, 64, 1), line1))
    for copy in row_got:
        copy.wait_recv()
    row_stat[2] = join_lse([row_stat[1]] + [row_in[3 + i] for i in range(3)])
    for place, (g0, k0), (g1, k1) in row_places:
        whole = row_stat[2, pl.ds(place, 1), :]
        for g, k in ((g0, k0), (g1, k1)):
            row_whole[g, k : k + 1, :] = whole
    for g in range(8):
        r = slice(g * 128, g * 128 + 128)
        row_scale[0, r, :], row_scale[1, r, :] = spread(jnp.exp2(row_local[g] - row_whole[g]))

    def weights(*tiles):
        for g in range(8):
            r = slice(g * 128, g * 128 + 128)
            learn_row, teach_row = row_scale[0, r, :], row_scale[1, r, :]
            for tile in tiles:
                c = slice(tile * 128, tile * 128 + 128)
                value = (by_row[0, r, c] * learn_row - by_row[1, r, c] * teach_row) + (
                    by_col[0, r, c] * col_scale[0:1, c] - by_col[1, r, c] * col_scale[1:2, c]
                )
                weight[r, c] = value.astype(BF16)

    text_got = {}

    def text_grads(*tiles):
        c = slice(tiles[0] * 128, tiles[-1] * 128 + 128)
        part = tn_dot(weight[:, c], img[:, :ds]) * grad_scale
        for i, (k, sib) in enumerate(TEXT_BLOCKS[2 * tiles[0] : 2 * tiles[-1] + 2]):
            piece = part[i * 64 : i * 64 + 64, :]
            if sib:
                text_send[k] = piece.astype(BF16)
                text_got[k] = send(text_send.at[k], text_in.at[k], device(sibling=True))
            else:
                text_own[k] = piece

    def join_cores(*ks):
        for k in ks:
            text_got[k].wait_recv()
            text_own[k] = text_own[k] + text_in[k].astype(F32)

    image_got = {}

    def image_grads(g):
        r = slice(g * 128, g * 128 + 128)
        part = jnp.dot(weight[r, :], txt[:, :ds], preferred_element_type=F32) * grad_scale
        for k, (h, p, q) in enumerate(HALF_BLOCKS[g]):
            piece = part[k * 32 : k * 32 + 32, :]
            if q == 0:
                image_own[h, p * 32 : p * 32 + 32, :] = piece
            else:
                image_send[h, q - 1, p * 32 : p * 32 + 32, :] = piece.astype(BF16)

    def image_pass_on(q, first, last):
        for h in (0, 1):
            at = pl.ds(first * 32, (last - first) * 32)
            copy = send(image_send.at[h, q - 1, at], image_in.at[h, q - 1, at], along(h, 2, q))
            for p in range(first, last):
                image_got[h, p, q] = copy

    def join_images(*ps):
        for p in ps:
            at = slice(p * 32, p * 32 + 32)
            for h in (0, 1):
                for q in (1, 2, 3):
                    if image_got[h, p, q] is not None:
                        image_got[h, p, q].wait_recv()
                        for other in range(NX):
                            if other != p and image_got[h, other, q] is image_got[h, p, q]:
                                image_got[h, other, q] = None
                        image_got[h, p, q] = None
                total = image_own[h, at, :] + functools.reduce(
                    jnp.add, [image_in[h, i, at, :].astype(F32) for i in range(3)]
                )
                if p == 0:
                    image_sum[h] = total
                else:
                    image_send2[h, p - 1] = total.astype(BF16)
                    image_got2.append(send(image_send2.at[h, p - 1], image_in2.at[h, p - 1], along(h, 1, p)))

    weights(6, 7)
    text_grads(6, 7)
    weights(5)
    text_grads(5)
    weights(0, 1, 2, 3, 4)
    image_grads(7)
    image_pass_on(2, 2, 4)
    join_cores(3, 5, 4)
    for i, k in ((2, 3), (3, 5), (4, 4)):
        text_send2[i] = text_own[k].astype(BF16)
    merge = [
        send(text_send2.at[4, pl.ds(0, 32)], text_in2.at[4, pl.ds(0, 32)], device(dz=2)),
        send(text_send2.at[4, pl.ds(32, 32)], text_in2.at[4, pl.ds(32, 32)], device(dz=-2)),
        send(text_send2.at[2], text_in2.at[2], device(dz=1)),
        send(text_send2.at[3], text_in2.at[3], device(dz=-1)),
    ]
    image_grads(6)
    image_pass_on(2, 0, 2)
    image_grads(5)
    image_grads(4)
    image_pass_on(1, 2, 4)
    image_pass_on(3, 2, 4)
    image_grads(3)
    image_pass_on(1, 1, 2)
    image_pass_on(3, 1, 2)
    image_grads(2)
    image_pass_on(3, 0, 1)
    image_grads(1)
    image_pass_on(1, 0, 1)
    text_grads(1, 2)
    text_grads(3, 4)
    text_grads(0)
    image_grads(0)
    join_cores(1, 7)
    for i, k in ((0, 1), (1, 7)):
        text_send2[i] = text_own[k].astype(BF16)
    final = [
        send(text_send2.at[0], text_in2.at[0], device(dz=1)),
        send(text_send2.at[1], text_in2.at[1], device(dz=-1)),
    ]
    join_cores(2, 6)
    image_got2 = []
    for copy in merge:
        copy.wait_recv()
    for i, k, h in ((0, 2, 0), (1, 6, 1)):
        joined = text_own[k] + text_in2[2 + i].astype(F32)
        near = slice(h * 32, h * 32 + 32)
        far = slice(32 - h * 32, 64 - h * 32)
        text_send3[i, near, :] = (joined[near] + text_in2[4, near, :].astype(F32)).astype(BF16)
        text_send3[i, far, :] = joined[far].astype(BF16)
        final.append(send(text_send3.at[i], text_in3.at[i], device(dz=2 - 4 * i)))
    join_images(2, 3, 1, 0)
    join_cores(0)
    for copy in image_got2:
        copy.wait_recv()
    for h in (0, 1):
        at = slice(h * 32, h * 32 + 32)
        total = image_sum[h] + functools.reduce(jnp.add, [image_in2[h, i].astype(F32) for i in range(3)])
        image_out[at, :] = back_norm(total, si_ref[at, :])
    for copy in final:
        copy.wait_recv()
    total = text_own[0]
    for ref in (text_in2, text_in3):
        total = total + ref[0].astype(F32) + ref[1].astype(F32)
    text_out[...] = back_norm(total, st_ref[...])
    for copy in copies:
        copy.wait_send()


def body(student_image, student_text, teacher_image, teacher_text, teacher_scale, student_scale):
    own, ds = student_image.shape
    width = ds + teacher_image.shape[1]
    vmem = pl.BlockSpec(memory_space=pltpu.VMEM)
    smem = pl.BlockSpec(memory_space=pltpu.SMEM)
    hbm = pl.BlockSpec(memory_space=pltpu.HBM)
    out = jax.ShapeDtypeStruct((own, ds), F32)
    return pl.pallas_call(
        kernel,
        out_shape=(out, out),
        in_specs=[smem, smem, hbm, hbm, hbm, hbm],
        out_specs=(vmem, vmem),
        scratch_shapes=[
            pltpu.VMEM((own, ds), BF16),
            pltpu.VMEM((own, ds), BF16),
            pltpu.VMEM((own, width - ds), BF16),
            pltpu.VMEM((own, width - ds), BF16),
            pltpu.VMEM((1024, width), BF16),
            pltpu.VMEM((1024, width), BF16),
            pltpu.VMEM((1024, 1024), F32),
            pltpu.VMEM((1024, 1024), F32),
            pltpu.VMEM((1024, 1024), BF16),
            pltpu.VMEM((4, 8, 4, 128), F32),
            pltpu.VMEM((8, 2, 1024), F32),
            pltpu.VMEM((3, 16, 128), F32),
            pltpu.VMEM((3, 16, 128), F32),
            pltpu.VMEM((6, 16, 128), F32),
            pltpu.VMEM((8, 16, 128), F32),
            pltpu.VMEM((8, 4, 128), F32),
            pltpu.VMEM((2, 1024), F32),
            pltpu.VMEM((8, 4, 128), F32),
            pltpu.VMEM((2, 1024, 128), F32),
            pltpu.VMEM((2, 1024), F32),
            pltpu.VMEM((2, 1024, 1024), F32),
            pltpu.VMEM((2, 1024, 1024), F32),
            pltpu.VMEM((2, 128, ds), F32),
            pltpu.VMEM((2, 3, 128, ds), BF16),
            pltpu.VMEM((2, 3, 128, ds), BF16),
            pltpu.VMEM((2, 32, ds), F32),
            pltpu.VMEM((2, 3, 32, ds), BF16),
            pltpu.VMEM((2, 3, 32, ds), BF16),
            pltpu.VMEM((NZ, 64, ds), F32),
            pltpu.VMEM((NZ, 64, ds), BF16),
            pltpu.VMEM((NZ, 64, ds), BF16),
            pltpu.VMEM((5, 64, ds), BF16),
            pltpu.VMEM((5, 64, ds), BF16),
            pltpu.VMEM((2, 64, ds), BF16),
            pltpu.VMEM((2, 64, ds), BF16),
            pltpu.SemaphoreType.DMA((COPIES,)),
            pltpu.SemaphoreType.DMA((COPIES,)),
            pltpu.SemaphoreType.DMA((4,)),
        ],
        compiler_params=pltpu.CompilerParams(
            collective_id=0, has_side_effects=True, vmem_limit_bytes=60 * 1024 * 1024
        ),
    )(
        teacher_scale.reshape(1, 1), student_scale.reshape(1, 1),
        student_image, student_text, teacher_image, teacher_text,
    )


def solution(mesh):
    placed = P(("row", "col"), None)
    return jax.shard_map(
        body,
        mesh=mesh,
        in_specs=(placed, placed, placed, placed, P(), P()),
        out_specs=(placed, placed),
        check_vma=False,
    )
```

```python
import functools
import math

import jax
import jax.numpy as jnp
from jax import lax
from jax.experimental import pallas as pl
from jax.experimental.pallas import tpu as pltpu
from jax.sharding import PartitionSpec as P

EPSILON = 1e-12
MESH = pl.DeviceIdType.MESH
NX, NY, NZ = 4, 4, 8
LOG2E = math.log2(math.e)
F32, BF16 = jnp.float32, jnp.bfloat16
SEMAPHORES = 64

PAIRS = (
    ((0, 0), (1, 0)),
    ((3, 0), (0, 1)),
    ((0, 3), (2, 0)),
    ((1, 1), (1, 3)),
    ((3, 1), (3, 3)),
    ((2, 1), (2, 3)),
    ((0, 2), (1, 2)),
    ((3, 2), (2, 2)),
)
HALF_BLOCKS = tuple(tuple((h, p, q) for h in (0, 1) for p, q in pair) for pair in PAIRS)
IMAGE_ROW = {key: g * 128 + k * 32 for g, keys in enumerate(HALF_BLOCKS) for k, key in enumerate(keys)}
TEXT_BLOCKS = (
    (0, 0), (0, 1), (1, 0), (7, 0), (1, 1), (7, 1),
    (2, 0), (6, 0), (2, 1), (6, 1),
    (3, 0), (5, 0), (3, 1), (5, 1),
    (4, 0), (4, 1),
)
TEXT_ROW = {key: i * 64 for i, key in enumerate(TEXT_BLOCKS)}
COLUMNS = ((0, 384), (384, 640), (640, 896), (896, 1024))


def unit_rows(raw):
    values = raw.astype(F32)
    inverse = lax.rsqrt(jnp.sum(values * values, axis=-1, keepdims=True) + EPSILON)
    return values * inverse, inverse


def join_lse(parts):
    top = functools.reduce(jnp.maximum, parts)
    total = functools.reduce(jnp.add, [jnp.exp2(part - top) for part in parts])
    return top + jnp.log(total) * LOG2E


def back_norm(grad, raw):
    unit, inverse = unit_rows(raw)
    return inverse * (grad - unit * jnp.sum(unit * grad, axis=-1, keepdims=True))


def nt_dot(a, b):
    return lax.dot_general(a, b, (((1,), (1,)), ((), ())), preferred_element_type=F32)


def tn_dot(a, b):
    return lax.dot_general(a, b, (((0,), (0,)), ((), ())), preferred_element_type=F32)


def kernel(
    tscale_ref, sscale_ref, si_hbm, st_hbm, ti_hbm, tt_hbm, grads_out,
    si_ref, st_ref, ti_ref, tt_ref, img, txt, teach, learn, weight, row_part, col_part, row_stat, col_stat, row_in, col_in,
    row_local, col_local, row_whole, row_scale, col_scale, by_row, by_col,
    image_own, image_send, image_in, image_sum, image_send2, image_in2,
    text_own, text_send, text_in, text_send2, text_in2, text_send3, text_in3,
    sem,
):
    ds = si_ref.shape[1]
    row, col = lax.axis_index("row"), lax.axis_index("col")
    y, core = row // 2, row % 2
    z, x = col // NX, col % NX

    def device(dx=0, dy=0, dz=0, sibling=False):
        c = 1 - core if sibling else core
        return (((y + dy) % NY) * 2 + c, ((z + dz) % NZ) * NX + (x + dx) % NX)

    def along(half, axis, d):
        return device(dx=d) if (half == 0) == (axis == 1) else device(dy=d)

    names = []

    def semaphore(*name):
        if name not in names:
            names.append(name)
        return sem.at[names.index(name)]

    def send(src, dst, target, leaves, lands):
        pltpu.make_async_remote_copy(
            src_ref=src, dst_ref=dst, send_sem=semaphore("leaves", leaves), recv_sem=semaphore(*lands),
            device_id=target, device_id_type=MESH,
        ).start()

    def wait(ref, *name):
        pltpu.make_async_copy(ref, ref, semaphore(*name)).wait()

    loads = [
        pltpu.make_async_copy(src, dst, semaphore("load", i))
        for i, (src, dst) in enumerate(((tt_hbm, tt_ref), (st_hbm, st_ref), (ti_hbm, ti_ref), (si_hbm, si_ref)))
    ]
    for load in loads:
        load.start()
    barrier = pltpu.get_barrier_semaphore()
    peers = [device(dx=1), device(dx=-1), device(dy=1), device(dy=-1), device(dz=1), device(dz=-1)]
    peers += [device(sibling=True)]
    for peer in peers:
        pl.semaphore_signal(barrier, inc=1, device_id=peer, device_id_type=MESH)
    for load in loads:
        load.wait()

    own_text = TEXT_ROW[(0, 0)]
    for start, size in ((0, 32), (32, 32)):
        for h_ref, lo, hi in ((si_ref, 0, ds), (ti_ref, ds, img.shape[1])):
            at = IMAGE_ROW[(start // 32, 0, 0)]
            img[at : at + size, lo:hi] = unit_rows(h_ref[start : start + size, :])[0].astype(BF16)
    for h_ref, lo, hi in ((st_ref, 0, ds), (tt_ref, ds, img.shape[1])):
        txt[own_text : own_text + 64, lo:hi] = unit_rows(h_ref[...])[0].astype(BF16)

    pl.semaphore_wait(barrier, len(peers))

    def rows(ref, at, size):
        return ref.at[pl.ds(at, size), :]

    def text_rows(k, part, size=16, sib=0):
        return rows(txt, TEXT_ROW[(k, sib)] + part * size, size)

    def image_rows(h, p, q, part=None):
        at = IMAGE_ROW[(h, p, q)]
        return rows(img, at, 32) if part is None else rows(img, at + part * 16, 16)

    def image_on(h, p, q, to, axis, d, lands, part=None):
        send(image_rows(h, p, q, part), image_rows(h, *to, part), along(h, axis, d), "image", lands)

    def to_second_axis(h, p):
        image_on(h, p, 0, (p, 1), 2, -1, ("image", p, 1))
        image_on(h, p, 0, (p, 3), 2, 1, ("image", p, 3))

    def text_on(k, j, part, d, lands):
        send(text_rows(k, part), text_rows(j, part), device(dz=d), "text", lands)

    def text_to_sibling(k, half, lands):
        send(text_rows(k, half, 32), text_rows(k, half, 32, 1), device(sibling=True), "text", ("sibling", lands))

    def text_arrive(k, step):
        wait(rows(txt, 0, 32), "text", k, step)
        for slot, part, d in ((k, step, -1), (NZ - k, 3 - step, 1)):
            if k < 3 or step < 2:
                text_on(slot, slot - d if k < 3 else 4, part, d, ("text", k + 1, step))
            if step % 2:
                text_to_sibling(slot, part // 2, k if k > 1 else 0)

    def text_arrive_last(step):
        wait(rows(txt, 0, 32), "text", 4, step)
        if step == 1:
            for half in (0, 1):
                text_to_sibling(4, half, 4)

    def sibling_arrive(first, blocks):
        wait(rows(txt, 0, blocks * 64), "sibling", first)

    def first_axis_arrive():
        for p, part, d in ((1, 0, -1), (3, 1, 1)):
            wait(rows(img, 0, 64), "image", p, 0)
            for h in (0, 1):
                image_on(h, p, 0, (2, 0), 1, d, ("image", 2, 0), part)
        for p in (1, 3):
            for h in (0, 1):
                to_second_axis(h, p)

    def second_axis_arrive(p):
        for q, part, d in ((1, 0, -1), (3, 1, 1)):
            wait(rows(img, 0, 64), "image", p, q)
            for h in (0, 1):
                image_on(h, p, q, (p, 2), 2, d, ("image", "last"), part)

    teach_scale = tscale_ref[0, 0] * LOG2E
    learn_scale = sscale_ref[0, 0] * LOG2E
    lane = lax.broadcasted_iota(jnp.int32, (128, 128), 1)
    line = lax.broadcasted_iota(jnp.int32, (128, 128), 0)
    spot = line % 32 + 32 * (line // 64)
    learn_spot = lane == spot
    teach_spot = lane == spot + 64

    def logits(first, last, *blocks):
        r = slice(first * 128, last * 128)
        for b in blocks:
            c = slice(*COLUMNS[b])
            for ref, lo, hi, scale in ((learn, 0, ds, learn_scale), (teach, ds, img.shape[1], teach_scale)):
                ref[r, c] = nt_dot(img[r, lo:hi], txt[c, lo:hi]) * scale

        for g in range(first, last):
            r = g * 128
            for b in blocks:
                c = slice(*COLUMNS[b])
                row_ls = []
                for i, ref in enumerate((learn, teach)):
                    block = ref[pl.ds(r, 128), c]
                    top = jnp.max(block, axis=1, keepdims=True)
                    total = jnp.sum(jnp.exp2(block - top), axis=1, keepdims=True)
                    row_ls.append(top + jnp.log(total) * LOG2E)
                    top = jnp.max(block, axis=0, keepdims=True)
                    total = jnp.sum(jnp.exp2(block - top), axis=0, keepdims=True)
                    col_part[g, i : i + 1, c] = top + jnp.log(total) * LOG2E
                packed = jnp.where(learn_spot, row_ls[0], 0.0) + jnp.where(teach_spot, row_ls[1], 0.0)
                row_part[b, g] = jnp.sum(packed.reshape(4, 32, 128), axis=1)

    for step in range(4):
        text_on(0, 1, step, -1, ("text", 1, step))
        text_on(0, 7, 3 - step, 1, ("text", 1, step))
        if step == 0:
            for h in (0, 1):
                image_on(h, 0, 0, (1, 0), 1, -1, ("image", 1, 0))
                image_on(h, 0, 0, (3, 0), 1, 1, ("image", 3, 0))
    for h in (0, 1):
        to_second_axis(h, 0)
    for half in (0, 1):
        text_to_sibling(0, half, 0)

    text_arrive(1, 0)
    first_axis_arrive()
    text_arrive(1, 1)
    text_arrive(1, 2)
    text_arrive(1, 3)
    second_axis_arrive(0)
    wait(rows(img, 0, 64), "image", 2, 0)
    for h in (0, 1):
        to_second_axis(h, 2)
    text_arrive(2, 0)
    sibling_arrive(0, 3)
    logits(0, 3, 0)
    text_arrive(2, 1)
    second_axis_arrive(1)
    text_arrive(2, 2)
    logits(3, 4, 0)
    text_arrive(2, 3)
    second_axis_arrive(3)
    text_arrive(3, 0)
    logits(4, 5, 0)
    sibling_arrive(2, 2)
    logits(0, 3, 1)
    text_arrive(3, 1)
    logits(3, 5, 1)
    text_arrive(3, 2)
    second_axis_arrive(2)
    text_arrive(3, 3)
    logits(5, 6, 0, 1)
    text_arrive_last(0)
    sibling_arrive(3, 2)
    logits(0, 6, 2)
    text_arrive_last(1)
    wait(rows(img, 0, 256), "image", "last")
    logits(6, 8, 0, 1, 2)
    sibling_arrive(4, 1)
    logits(0, 8, 3)

    low = lax.broadcasted_iota(jnp.int32, (1, 128), 1) < 64
    half0 = lax.broadcasted_iota(jnp.int32, (1, 128), 1) % 64 < 32
    where_is = {key: (g, k) for g, keys in enumerate(HALF_BLOCKS) for k, key in enumerate(keys)}
    row_places = [
        (((y + dy) % NY) * NX + (x + dx) % NX, where_is[0, dx, dy], where_is[1, dy, dx])
        for dy in range(NY)
        for dx in range(NX)
    ]
    col_places = [(1 - core if sib else core) * NZ + (z + k) % NZ for k, sib in TEXT_BLOCKS]

    def spread(lines):
        lines = jnp.broadcast_to(lines[:, None, :], (4, 32, 128)).reshape(128, 128)
        for mask in (learn_spot, teach_spot):
            yield jnp.broadcast_to(jnp.sum(jnp.where(mask, lines, 0.0), axis=1, keepdims=True), (128, 128))

    col_local[...] = join_lse([col_part[g] for g in range(8)])
    for tile in range(8):
        c = slice(tile * 128, tile * 128 + 128)
        ls, lt = col_local[0:1, c], col_local[1:2, c]
        first, second = col_places[2 * tile : 2 * tile + 2]
        col_stat[0, pl.ds(first, 1), :] = jnp.where(low, ls, pltpu.roll(lt, 64, 1))
        col_stat[0, pl.ds(second, 1), :] = jnp.where(low, pltpu.roll(ls, 64, 1), lt)
    send(col_stat.at[0], col_in.at[0], device(sibling=True), "cols", ("col", 0))
    row_local[...] = join_lse([row_part[b] for b in range(len(COLUMNS))])
    for place, (g0, k0), (g1, k1) in row_places:
        row_stat[0, pl.ds(place, 1), :] = jnp.where(half0, row_local[g0, k0 : k0 + 1, :], row_local[g1, k1 : k1 + 1, :])
    for d in (2, 1, 3):
        send(row_stat.at[0], row_in.at[d - 1], device(dx=d), "rows", ("row", 0))

    def local_softmax(*groups):
        for g in groups:
            r = slice(g * 128, g * 128 + 128)
            row_ls = list(spread(row_local[g]))
            for tile in range(8):
                c = slice(tile * 128, tile * 128 + 128)
                for i, ref in enumerate((learn, teach)):
                    block = ref[r, c] - 1.0
                    by_row[i, r, c] = jnp.exp2(block - row_ls[i])
                    by_col[i, r, c] = jnp.exp2(block - col_local[i : i + 1, c])

    local_softmax(0, 1)
    wait(col_in.at[0], "col", 0)
    col_stat[1] = join_lse([col_stat[0], col_in[0]])
    for d in (4, 3, 5, 2, 6, 1, 7):
        send(col_stat.at[1], col_in.at[d], device(dz=d), "cols", ("col", 1))
    local_softmax(2, 3, 4)
    wait(row_in.at[pl.ds(0, 3)], "row", 0)
    row_stat[1] = join_lse([row_stat[0]] + [row_in[i] for i in range(3)])
    for d in (2, 1, 3):
        send(row_stat.at[1], row_in.at[2 + d], device(dy=d), "rows", ("row", 1))
    local_softmax(5, 6, 7)
    wait(col_in.at[pl.ds(1, NZ - 1)], "col", 1)
    col_stat[2] = join_lse([col_stat[1]] + [col_in[d] for d in range(1, NZ)])
    for tile in range(8):
        c = slice(tile * 128, tile * 128 + 128)
        first, second = col_places[2 * tile : 2 * tile + 2]
        line0 = col_stat[2, pl.ds(first, 1), :]
        line1 = col_stat[2, pl.ds(second, 1), :]
        col_scale[0:1, c] = jnp.exp2(col_local[0:1, c] - jnp.where(low, line0, pltpu.roll(line1, 64, 1)))
        col_scale[1:2, c] = jnp.exp2(col_local[1:2, c] - jnp.where(low, pltpu.roll(line0, 64, 1), line1))
    wait(row_in.at[pl.ds(3, 3)], "row", 1)
    row_stat[2] = join_lse([row_stat[1]] + [row_in[3 + i] for i in range(3)])
    for place, (g0, k0), (g1, k1) in row_places:
        whole = row_stat[2, pl.ds(place, 1), :]
        for g, k in ((g0, k0), (g1, k1)):
            row_whole[g, k : k + 1, :] = whole
    for g in range(8):
        r = slice(g * 128, g * 128 + 128)
        row_scale[0, r, :], row_scale[1, r, :] = spread(jnp.exp2(row_local[g] - row_whole[g]))

    def weights(*tiles):
        for g in range(8):
            r = slice(g * 128, g * 128 + 128)
            learn_row, teach_row = row_scale[0, r, :], row_scale[1, r, :]
            for tile in tiles:
                c = slice(tile * 128, tile * 128 + 128)
                value = (by_row[0, r, c] * learn_row - by_row[1, r, c] * teach_row) + (
                    by_col[0, r, c] * col_scale[0:1, c] - by_col[1, r, c] * col_scale[1:2, c]
                )
                weight[r, c] = value.astype(BF16)

    def text_grads(*tiles):
        c = slice(tiles[0] * 128, tiles[-1] * 128 + 128)
        part = tn_dot(weight[:, c], img[:, :ds])
        for i, (k, sib) in enumerate(TEXT_BLOCKS[2 * tiles[0] : 2 * tiles[-1] + 2]):
            piece = part[i * 64 : i * 64 + 64, :]
            if sib:
                text_send[k] = piece.astype(BF16)
                lands = ("joined", min(k, NZ - k))
                send(text_send.at[k], text_in.at[k], device(sibling=True), "joined", lands)
            else:
                text_own[k] = piece

    def join_cores(*ks):
        for first in sorted({min(k, NZ - k) for k in ks}):
            wait(text_in.at[pl.ds(0, 1 if first in (0, 4) else 2)], "joined", first)
        for k in ks:
            text_own[k] = text_own[k] + text_in[k].astype(F32)

    def image_grads(g):
        r = slice(g * 128, g * 128 + 128)
        part = jnp.dot(weight[r, :], txt[:, :ds], preferred_element_type=F32)
        for k, (h, p, q) in enumerate(HALF_BLOCKS[g]):
            piece = part[k * 32 : k * 32 + 32, :]
            if q == 0:
                image_own[h, p * 32 : p * 32 + 32, :] = piece
            else:
                image_send[h, q - 1, p * 32 : p * 32 + 32, :] = piece.astype(BF16)

    def image_pass_on(q, first, last):
        at = pl.ds(first * 32, (last - first) * 32)
        for h in (0, 1):
            send(image_send.at[h, q - 1, at], image_in.at[h, q - 1, at], along(h, 2, q), "parts", ("parts", first))

    def join_images(first, last):
        wait(image_in.at[:, :, pl.ds(first * 32, (last - first) * 32)], "parts", first)
        for p in range(first, last):
            at = slice(p * 32, p * 32 + 32)
            for h in (0, 1):
                total = image_own[h, at, :] + functools.reduce(
                    jnp.add, [image_in[h, i, at, :].astype(F32) for i in range(3)]
                )
                if p == 0:
                    image_sum[h] = total
                else:
                    image_send2[h, p - 1] = total.astype(BF16)
                    send(image_send2.at[h, p - 1], image_in2.at[h, p - 1], along(h, 1, p), "sums", ("sums",))

    def text_pass_on(src, dst, d, lands):
        send(src, dst, device(dz=d), "text sums", (lands,))

    weights(6, 7)
    text_grads(6, 7)
    weights(5)
    text_grads(5)
    weights(0, 1, 2, 3, 4)
    image_grads(7)
    image_pass_on(2, 2, 4)
    join_cores(3, 5, 4)
    for i, k in ((2, 3), (3, 5), (4, 4)):
        text_send2[i] = text_own[k].astype(BF16)
    for h, d in ((0, 2), (1, -2)):
        at = pl.ds(h * 32, 32)
        text_pass_on(text_send2.at[4, at], text_in2.at[4, at], d, "merge")
    text_pass_on(text_send2.at[2], text_in2.at[2], 1, "merge")
    text_pass_on(text_send2.at[3], text_in2.at[3], -1, "merge")
    image_grads(5)
    image_grads(4)
    image_pass_on(1, 2, 4)
    image_pass_on(3, 2, 4)
    image_grads(6)
    image_pass_on(2, 1, 2)
    image_grads(3)
    image_pass_on(1, 1, 2)
    image_pass_on(3, 1, 2)
    image_pass_on(2, 0, 1)
    image_grads(2)
    image_pass_on(3, 0, 1)
    image_grads(1)
    image_pass_on(1, 0, 1)
    text_grads(1, 2)
    text_grads(3, 4)
    text_grads(0)
    image_grads(0)
    join_cores(1, 7)
    for i, k in ((0, 1), (1, 7)):
        text_send2[i] = text_own[k].astype(BF16)
    text_pass_on(text_send2.at[0], text_in2.at[0], 1, "final")
    text_pass_on(text_send2.at[1], text_in2.at[1], -1, "final")
    join_cores(2, 6)
    join_cores(0)
    wait(text_in2.at[pl.ds(2, 3)], "merge")
    for i, k, h in ((0, 2, 0), (1, 6, 1)):
        joined = text_own[k] + text_in2[2 + i].astype(F32)
        near = slice(h * 32, h * 32 + 32)
        far = slice(32 - h * 32, 64 - h * 32)
        text_send3[i, near, :] = (joined[near] + text_in2[4, near, :].astype(F32)).astype(BF16)
        text_send3[i, far, :] = joined[far].astype(BF16)
        text_pass_on(text_send3.at[i], text_in3.at[i], 2 - 4 * i, "final")
    join_images(2, 4)
    join_images(1, 2)
    join_images(0, 1)
    wait(image_in2, "sums")
    for h in (0, 1):
        at = slice(h * 32, h * 32 + 32)
        total = image_sum[h] + functools.reduce(jnp.add, [image_in2[h, i].astype(F32) for i in range(3)])
        grads_out[0, at, :] = back_norm(total, si_ref[at, :])
    wait(text_in.at[pl.ds(0, 4)], "final")
    total = text_own[0]
    for ref in (text_in2, text_in3):
        total = total + ref[0].astype(F32) + ref[1].astype(F32)
    grads_out[1] = back_norm(total, st_ref[...])
    wait(rows(img, 0, 960), "leaves", "image")
    wait(rows(txt, 0, 960), "leaves", "text")
    wait(row_in, "leaves", "rows")
    wait(col_in, "leaves", "cols")
    wait(image_send, "leaves", "parts")
    wait(image_send2, "leaves", "sums")
    wait(text_send, "leaves", "joined")
    wait(text_send.at[pl.ds(0, 7)], "leaves", "text sums")


def body(student_image, student_text, teacher_image, teacher_text, teacher_scale, student_scale):
    own, ds = student_image.shape
    width = ds + teacher_image.shape[1]
    vmem = pl.BlockSpec(memory_space=pltpu.VMEM)
    smem = pl.BlockSpec(memory_space=pltpu.SMEM)
    hbm = pl.BlockSpec(memory_space=pltpu.HBM)
    grads = pl.pallas_call(
        kernel,
        out_shape=jax.ShapeDtypeStruct((2, own, ds), F32),
        in_specs=[smem, smem, hbm, hbm, hbm, hbm],
        out_specs=vmem,
        scratch_shapes=[
            pltpu.VMEM((own, ds), BF16),
            pltpu.VMEM((own, ds), BF16),
            pltpu.VMEM((own, width - ds), BF16),
            pltpu.VMEM((own, width - ds), BF16),
            pltpu.VMEM((1024, width), BF16),
            pltpu.VMEM((1024, width), BF16),
            pltpu.VMEM((1024, 1024), F32),
            pltpu.VMEM((1024, 1024), F32),
            pltpu.VMEM((1024, 1024), BF16),
            pltpu.VMEM((4, 8, 4, 128), F32),
            pltpu.VMEM((8, 2, 1024), F32),
            pltpu.VMEM((3, 16, 128), F32),
            pltpu.VMEM((3, 16, 128), F32),
            pltpu.VMEM((6, 16, 128), F32),
            pltpu.VMEM((8, 16, 128), F32),
            pltpu.VMEM((8, 4, 128), F32),
            pltpu.VMEM((2, 1024), F32),
            pltpu.VMEM((8, 4, 128), F32),
            pltpu.VMEM((2, 1024, 128), F32),
            pltpu.VMEM((2, 1024), F32),
            pltpu.VMEM((2, 1024, 1024), F32),
            pltpu.VMEM((2, 1024, 1024), F32),
            pltpu.VMEM((2, 128, ds), F32),
            pltpu.VMEM((2, 3, 128, ds), BF16),
            pltpu.VMEM((2, 3, 128, ds), BF16),
            pltpu.VMEM((2, 32, ds), F32),
            pltpu.VMEM((2, 3, 32, ds), BF16),
            pltpu.VMEM((2, 3, 32, ds), BF16),
            pltpu.VMEM((NZ, 64, ds), F32),
            pltpu.VMEM((NZ, 64, ds), BF16),
            pltpu.VMEM((NZ, 64, ds), BF16),
            pltpu.VMEM((5, 64, ds), BF16),
            pltpu.VMEM((5, 64, ds), BF16),
            pltpu.VMEM((2, 64, ds), BF16),
            pltpu.VMEM((2, 64, ds), BF16),
            pltpu.SemaphoreType.DMA((SEMAPHORES,)),
        ],
        compiler_params=pltpu.CompilerParams(
            collective_id=0, has_side_effects=True, vmem_limit_bytes=60 * 1024 * 1024
        ),
    )(
        teacher_scale.reshape(1, 1), student_scale.reshape(1, 1),
        student_image, student_text, teacher_image, teacher_text,
    )
    return grads[0] * student_scale, grads[1] * student_scale


def solution(mesh):
    placed = P(("row", "col"), None)
    return jax.shard_map(
        body,
        mesh=mesh,
        in_specs=(placed, placed, placed, placed, P(), P()),
        out_specs=(placed, placed),
        check_vma=False,
    )
```

```python
import functools
import math

import jax
import jax.numpy as jnp
from jax import lax
from jax.experimental import pallas as pl
from jax.experimental.pallas import tpu as pltpu
from jax.sharding import PartitionSpec as P

EPSILON = 1e-12
MESH = pl.DeviceIdType.MESH
NX, NY, NZ = 4, 4, 8
LOG2E = math.log2(math.e)
F32, BF16 = jnp.float32, jnp.bfloat16
SEMAPHORES = 64

PAIRS = (
    ((0, 0), (1, 0)),
    ((3, 0), (0, 1)),
    ((0, 3), (2, 0)),
    ((1, 1), (1, 3)),
    ((3, 1), (3, 3)),
    ((2, 1), (2, 3)),
    ((0, 2), (1, 2)),
    ((3, 2), (2, 2)),
)
HALF_BLOCKS = tuple(tuple((h, p, q) for h in (0, 1) for p, q in pair) for pair in PAIRS)
IMAGE_ROW = {key: g * 128 + k * 32 for g, keys in enumerate(HALF_BLOCKS) for k, key in enumerate(keys)}
TEXT_BLOCKS = (
    (0, 0), (0, 1), (1, 0), (7, 0), (1, 1), (7, 1),
    (2, 0), (6, 0), (2, 1), (6, 1),
    (3, 0), (5, 0), (3, 1), (5, 1),
    (4, 0), (4, 1),
)
TEXT_ROW = {key: i * 64 for i, key in enumerate(TEXT_BLOCKS)}
COLUMNS = ((0, 384), (384, 640), (640, 896), (896, 1024))


def unit_rows(raw):
    values = raw.astype(F32)
    inverse = lax.rsqrt(jnp.sum(values * values, axis=-1, keepdims=True) + EPSILON)
    return values * inverse, inverse


def join_lse(parts):
    top = functools.reduce(jnp.maximum, parts)
    total = functools.reduce(jnp.add, [jnp.exp2(part - top) for part in parts])
    return top + jnp.log(total) * LOG2E


def back_norm(grad, raw):
    unit, inverse = unit_rows(raw)
    return inverse * (grad - unit * jnp.sum(unit * grad, axis=-1, keepdims=True))


def nt_dot(a, b):
    return lax.dot_general(a, b, (((1,), (1,)), ((), ())), preferred_element_type=F32)


def tn_dot(a, b):
    return lax.dot_general(a, b, (((0,), (0,)), ((), ())), preferred_element_type=F32)


def kernel(
    tscale_ref, sscale_ref, si_hbm, st_hbm, ti_hbm, tt_hbm, grads_out,
    si_ref, st_ref, ti_ref, tt_ref, img, txt, teach, learn, weight, row_part, col_part, row_stat, col_stat, row_in, col_in,
    row_local, col_local, row_whole, row_scale, col_scale, by_row, by_col,
    image_own, image_send, image_in, image_sum, image_send2, image_in2,
    text_own, text_send, text_in, text_send2, text_in2, text_send3, text_in3,
    sem,
):
    ds = si_ref.shape[1]
    row, col = lax.axis_index("row"), lax.axis_index("col")
    y, core = row // 2, row % 2
    z, x = col // NX, col % NX

    def device(dx=0, dy=0, dz=0, sibling=False):
        c = 1 - core if sibling else core
        return (((y + dy) % NY) * 2 + c, ((z + dz) % NZ) * NX + (x + dx) % NX)

    def along(half, axis, d):
        return device(dx=d) if (half == 0) == (axis == 1) else device(dy=d)

    names = []

    def semaphore(*name):
        if name not in names:
            names.append(name)
        return sem.at[names.index(name)]

    def send(src, dst, target, leaves, lands):
        pltpu.make_async_remote_copy(
            src_ref=src, dst_ref=dst, send_sem=semaphore("leaves", leaves), recv_sem=semaphore(*lands),
            device_id=target, device_id_type=MESH,
        ).start()

    def wait(ref, *name):
        pltpu.make_async_copy(ref, ref, semaphore(*name)).wait()

    loads = [
        pltpu.make_async_copy(src, dst, semaphore("load", i))
        for i, (src, dst) in enumerate(((tt_hbm, tt_ref), (st_hbm, st_ref), (ti_hbm, ti_ref), (si_hbm, si_ref)))
    ]
    for load in loads:
        load.start()
    barrier = pltpu.get_barrier_semaphore()
    peers = [device(dx=1), device(dx=-1), device(dy=1), device(dy=-1), device(dz=1), device(dz=-1)]
    peers += [device(sibling=True)]
    for peer in peers:
        pl.semaphore_signal(barrier, inc=1, device_id=peer, device_id_type=MESH)
    for load in loads:
        load.wait()

    own_text = TEXT_ROW[(0, 0)]
    for start, size in ((0, 32), (32, 32)):
        for h_ref, lo, hi in ((si_ref, 0, ds), (ti_ref, ds, img.shape[1])):
            at = IMAGE_ROW[(start // 32, 0, 0)]
            img[at : at + size, lo:hi] = unit_rows(h_ref[start : start + size, :])[0].astype(BF16)
    for h_ref, lo, hi in ((st_ref, 0, ds), (tt_ref, ds, img.shape[1])):
        txt[own_text : own_text + 64, lo:hi] = unit_rows(h_ref[...])[0].astype(BF16)

    pl.semaphore_wait(barrier, len(peers))

    def rows(ref, at, size):
        return ref.at[pl.ds(at, size), :]

    def text_rows(k, part, size=16, sib=0):
        return rows(txt, TEXT_ROW[(k, sib)] + part * size, size)

    def image_rows(h, p, q, part=None):
        at = IMAGE_ROW[(h, p, q)]
        return rows(img, at, 32) if part is None else rows(img, at + part * 16, 16)

    def image_on(h, p, q, to, axis, d, lands, part=None):
        send(image_rows(h, p, q, part), image_rows(h, *to, part), along(h, axis, d), "image", lands)

    def to_second_axis(h, p):
        image_on(h, p, 0, (p, 1), 2, -1, ("image", p, 1))
        image_on(h, p, 0, (p, 3), 2, 1, ("image", p, 3))

    def text_on(k, j, part, d, lands):
        send(text_rows(k, part), text_rows(j, part), device(dz=d), "text", lands)

    def text_to_sibling(k, half, lands):
        send(text_rows(k, half, 32), text_rows(k, half, 32, 1), device(sibling=True), "text", ("sibling", lands))

    def text_arrive(k, step):
        wait(rows(txt, 0, 32), "text", k, step)
        for slot, part, d in ((k, step, -1), (NZ - k, 3 - step, 1)):
            if k < 3 or step < 2:
                text_on(slot, slot - d if k < 3 else 4, part, d, ("text", k + 1, step))
            if step % 2:
                text_to_sibling(slot, part // 2, k if k > 1 else 0)

    def text_arrive_last(step):
        wait(rows(txt, 0, 32), "text", 4, step)
        if step == 1:
            for half in (0, 1):
                text_to_sibling(4, half, 4)

    def sibling_arrive(first, blocks):
        wait(rows(txt, 0, blocks * 64), "sibling", first)

    def first_axis_arrive():
        for p, part, d in ((1, 0, -1), (3, 1, 1)):
            wait(rows(img, 0, 64), "image", p, 0)
            for h in (0, 1):
                image_on(h, p, 0, (2, 0), 1, d, ("image", 2, 0), part)
        for p in (1, 3):
            for h in (0, 1):
                to_second_axis(h, p)

    def second_axis_arrive(p):
        for q, part, d in ((1, 0, -1), (3, 1, 1)):
            wait(rows(img, 0, 64), "image", p, q)
            for h in (0, 1):
                image_on(h, p, q, (p, 2), 2, d, ("image", "last"), part)

    teach_scale = tscale_ref[0, 0] * LOG2E
    learn_scale = sscale_ref[0, 0] * LOG2E
    lane = lax.broadcasted_iota(jnp.int32, (128, 128), 1)
    line = lax.broadcasted_iota(jnp.int32, (128, 128), 0)
    spot = line % 32 + 32 * (line // 64)
    learn_spot = lane == spot
    teach_spot = lane == spot + 64

    def logits(first, last, *blocks):
        r = slice(first * 128, last * 128)
        for b in blocks:
            c = slice(*COLUMNS[b])
            for ref, lo, hi, scale in ((learn, 0, ds, learn_scale), (teach, ds, img.shape[1], teach_scale)):
                ref[r, c] = nt_dot(img[r, lo:hi], txt[c, lo:hi]) * scale

        for g in range(first, last):
            r = g * 128
            for b in blocks:
                c = slice(*COLUMNS[b])
                row_ls = []
                for i, ref in enumerate((learn, teach)):
                    block = ref[pl.ds(r, 128), c]
                    top = jnp.max(block, axis=1, keepdims=True)
                    total = jnp.sum(jnp.exp2(block - top), axis=1, keepdims=True)
                    row_ls.append(top + jnp.log(total) * LOG2E)
                    top = jnp.max(block, axis=0, keepdims=True)
                    total = jnp.sum(jnp.exp2(block - top), axis=0, keepdims=True)
                    col_part[g, i : i + 1, c] = top + jnp.log(total) * LOG2E
                packed = jnp.where(learn_spot, row_ls[0], 0.0) + jnp.where(teach_spot, row_ls[1], 0.0)
                row_part[b, g] = jnp.sum(packed.reshape(4, 32, 128), axis=1)

    for step in range(4):
        text_on(0, 1, step, -1, ("text", 1, step))
        text_on(0, 7, 3 - step, 1, ("text", 1, step))
        if step == 0:
            for h in (0, 1):
                image_on(h, 0, 0, (1, 0), 1, -1, ("image", 1, 0))
                image_on(h, 0, 0, (3, 0), 1, 1, ("image", 3, 0))
    for h in (0, 1):
        to_second_axis(h, 0)
    for half in (0, 1):
        text_to_sibling(0, half, 0)

    text_arrive(1, 0)
    first_axis_arrive()
    text_arrive(1, 1)
    text_arrive(1, 2)
    text_arrive(1, 3)
    second_axis_arrive(0)
    wait(rows(img, 0, 64), "image", 2, 0)
    for h in (0, 1):
        to_second_axis(h, 2)
    text_arrive(2, 0)
    sibling_arrive(0, 3)
    logits(0, 3, 0)
    text_arrive(2, 1)
    second_axis_arrive(1)
    text_arrive(2, 2)
    logits(3, 4, 0)
    text_arrive(2, 3)
    second_axis_arrive(3)
    text_arrive(3, 0)
    logits(4, 5, 0)
    sibling_arrive(2, 2)
    logits(0, 3, 1)
    text_arrive(3, 1)
    logits(3, 5, 1)
    text_arrive(3, 2)
    second_axis_arrive(2)
    text_arrive(3, 3)
    logits(5, 6, 0, 1)
    text_arrive_last(0)
    sibling_arrive(3, 2)
    logits(0, 6, 2)
    text_arrive_last(1)
    wait(rows(img, 0, 256), "image", "last")
    logits(6, 8, 0, 1, 2)
    sibling_arrive(4, 1)
    logits(0, 8, 3)

    low = lax.broadcasted_iota(jnp.int32, (1, 128), 1) < 64
    half0 = lax.broadcasted_iota(jnp.int32, (1, 128), 1) % 64 < 32
    where_is = {key: (g, k) for g, keys in enumerate(HALF_BLOCKS) for k, key in enumerate(keys)}
    row_places = [
        (((y + dy) % NY) * NX + (x + dx) % NX, where_is[0, dx, dy], where_is[1, dy, dx])
        for dy in range(NY)
        for dx in range(NX)
    ]
    col_places = [(1 - core if sib else core) * NZ + (z + k) % NZ for k, sib in TEXT_BLOCKS]

    def spread(lines):
        lines = jnp.broadcast_to(lines[:, None, :], (4, 32, 128)).reshape(128, 128)
        for mask in (learn_spot, teach_spot):
            yield jnp.broadcast_to(jnp.sum(jnp.where(mask, lines, 0.0), axis=1, keepdims=True), (128, 128))

    col_local[...] = join_lse([col_part[g] for g in range(8)])
    for tile in range(8):
        c = slice(tile * 128, tile * 128 + 128)
        ls, lt = col_local[0:1, c], col_local[1:2, c]
        first, second = col_places[2 * tile : 2 * tile + 2]
        col_stat[0, pl.ds(first, 1), :] = jnp.where(low, ls, pltpu.roll(lt, 64, 1))
        col_stat[0, pl.ds(second, 1), :] = jnp.where(low, pltpu.roll(ls, 64, 1), lt)
    send(col_stat.at[0], col_in.at[0], device(sibling=True), "cols", ("col", 0))
    row_local[...] = join_lse([row_part[b] for b in range(len(COLUMNS))])
    for place, (g0, k0), (g1, k1) in row_places:
        row_stat[0, pl.ds(place, 1), :] = jnp.where(half0, row_local[g0, k0 : k0 + 1, :], row_local[g1, k1 : k1 + 1, :])
    for d in (2, 1, 3):
        send(row_stat.at[0], row_in.at[d - 1], device(dx=d), "rows", ("row", 0))

    def local_softmax(*groups):
        for g in groups:
            r = slice(g * 128, g * 128 + 128)
            row_ls = list(spread(row_local[g]))
            for tile in range(8):
                c = slice(tile * 128, tile * 128 + 128)
                for i, ref in enumerate((learn, teach)):
                    block = ref[r, c] - 1.0
                    by_row[i, r, c] = jnp.exp2(block - row_ls[i])
                    by_col[i, r, c] = jnp.exp2(block - col_local[i : i + 1, c])

    local_softmax(0, 1)
    wait(col_in.at[0], "col", 0)
    col_stat[1] = join_lse([col_stat[0], col_in[0]])
    for d in (4, 3, 5, 2, 6, 1, 7):
        send(col_stat.at[1], col_in.at[d], device(dz=d), "cols", ("col", 1))
    local_softmax(2, 3, 4)
    wait(row_in.at[pl.ds(0, 3)], "row", 0)
    row_stat[1] = join_lse([row_stat[0]] + [row_in[i] for i in range(3)])
    for d in (2, 1, 3):
        send(row_stat.at[1], row_in.at[2 + d], device(dy=d), "rows", ("row", 1))
    local_softmax(5, 6, 7)
    wait(col_in.at[pl.ds(1, NZ - 1)], "col", 1)
    col_stat[2] = join_lse([col_stat[1]] + [col_in[d] for d in range(1, NZ)])
    for tile in range(8):
        c = slice(tile * 128, tile * 128 + 128)
        first, second = col_places[2 * tile : 2 * tile + 2]
        line0 = col_stat[2, pl.ds(first, 1), :]
        line1 = col_stat[2, pl.ds(second, 1), :]
        col_scale[0:1, c] = jnp.exp2(col_local[0:1, c] - jnp.where(low, line0, pltpu.roll(line1, 64, 1)))
        col_scale[1:2, c] = jnp.exp2(col_local[1:2, c] - jnp.where(low, pltpu.roll(line0, 64, 1), line1))
    wait(row_in.at[pl.ds(3, 3)], "row", 1)
    row_stat[2] = join_lse([row_stat[1]] + [row_in[3 + i] for i in range(3)])
    for place, (g0, k0), (g1, k1) in row_places:
        whole = row_stat[2, pl.ds(place, 1), :]
        for g, k in ((g0, k0), (g1, k1)):
            row_whole[g, k : k + 1, :] = whole
    for g in range(8):
        r = slice(g * 128, g * 128 + 128)
        row_scale[0, r, :], row_scale[1, r, :] = spread(jnp.exp2(row_local[g] - row_whole[g]))

    def weights(*tiles):
        for g in range(8):
            r = slice(g * 128, g * 128 + 128)
            learn_row, teach_row = row_scale[0, r, :], row_scale[1, r, :]
            for tile in tiles:
                c = slice(tile * 128, tile * 128 + 128)
                value = (by_row[0, r, c] * learn_row - by_row[1, r, c] * teach_row) + (
                    by_col[0, r, c] * col_scale[0:1, c] - by_col[1, r, c] * col_scale[1:2, c]
                )
                weight[r, c] = value.astype(BF16)

    def text_grads(*tiles):
        c = slice(tiles[0] * 128, tiles[-1] * 128 + 128)
        part = tn_dot(weight[:, c], img[:, :ds])
        for i, (k, sib) in enumerate(TEXT_BLOCKS[2 * tiles[0] : 2 * tiles[-1] + 2]):
            piece = part[i * 64 : i * 64 + 64, :]
            if sib:
                text_send[k] = piece.astype(BF16)
                lands = ("joined", min(k, NZ - k))
                send(text_send.at[k], text_in.at[k], device(sibling=True), "joined", lands)
            else:
                text_own[k] = piece

    def join_cores(*ks):
        for first in sorted({min(k, NZ - k) for k in ks}):
            wait(text_in.at[pl.ds(0, 1 if first in (0, 4) else 2)], "joined", first)
        for k in ks:
            text_own[k] = text_own[k] + text_in[k].astype(F32)

    def image_grads(g):
        r = slice(g * 128, g * 128 + 128)
        part = jnp.dot(weight[r, :], txt[:, :ds], preferred_element_type=F32)
        for k, (h, p, q) in enumerate(HALF_BLOCKS[g]):
            piece = part[k * 32 : k * 32 + 32, :]
            if q == 0:
                image_own[h, p * 32 : p * 32 + 32, :] = piece
            else:
                image_send[h, q - 1, p * 32 : p * 32 + 32, :] = piece.astype(BF16)

    def image_pass_on(q, first, last):
        at = pl.ds(first * 32, (last - first) * 32)
        for h in (0, 1):
            send(image_send.at[h, q - 1, at], image_in.at[h, q - 1, at], along(h, 2, q), "parts", ("parts", first))

    def join_images(first, last):
        wait(image_in.at[:, :, pl.ds(first * 32, (last - first) * 32)], "parts", first)
        for p in range(first, last):
            at = slice(p * 32, p * 32 + 32)
            for h in (0, 1):
                total = image_own[h, at, :] + functools.reduce(
                    jnp.add, [image_in[h, i, at, :].astype(F32) for i in range(3)]
                )
                if p == 0:
                    image_sum[h] = total
                else:
                    image_send2[h, p - 1] = total.astype(BF16)
                    send(image_send2.at[h, p - 1], image_in2.at[h, p - 1], along(h, 1, p), "sums", ("sums",))

    def text_pass_on(src, dst, d, lands):
        send(src, dst, device(dz=d), "text sums", (lands,))

    weights(6, 7)
    text_grads(6, 7)
    weights(5)
    text_grads(5)
    weights(0, 1, 2, 3, 4)
    image_grads(7)
    image_pass_on(2, 2, 4)
    join_cores(3, 5, 4)
    for i, k in ((2, 3), (3, 5), (4, 4)):
        text_send2[i] = text_own[k].astype(BF16)
    for h, d in ((0, 2), (1, -2)):
        at = pl.ds(h * 32, 32)
        text_pass_on(text_send2.at[4, at], text_in2.at[4, at], d, "merge")
    text_pass_on(text_send2.at[2], text_in2.at[2], 1, "merge")
    text_pass_on(text_send2.at[3], text_in2.at[3], -1, "merge")
    image_grads(5)
    image_grads(4)
    image_pass_on(1, 2, 4)
    image_pass_on(3, 2, 4)
    image_grads(6)
    image_pass_on(2, 1, 2)
    image_grads(3)
    image_pass_on(1, 1, 2)
    image_pass_on(3, 1, 2)
    image_pass_on(2, 0, 1)
    image_grads(2)
    image_pass_on(3, 0, 1)
    image_grads(1)
    image_pass_on(1, 0, 1)
    text_grads(1, 2)
    text_grads(3, 4)
    text_grads(0)
    image_grads(0)
    join_cores(1, 7)
    for i, k in ((0, 1), (1, 7)):
        text_send2[i] = text_own[k].astype(BF16)
    text_pass_on(text_send2.at[0], text_in2.at[0], 1, "final")
    text_pass_on(text_send2.at[1], text_in2.at[1], -1, "final")
    join_cores(2, 6)
    join_cores(0)
    wait(text_in2.at[pl.ds(2, 3)], "merge")
    for i, k, h in ((0, 2, 0), (1, 6, 1)):
        joined = text_own[k] + text_in2[2 + i].astype(F32)
        near = slice(h * 32, h * 32 + 32)
        far = slice(32 - h * 32, 64 - h * 32)
        text_send3[i, near, :] = (joined[near] + text_in2[4, near, :].astype(F32)).astype(BF16)
        text_send3[i, far, :] = joined[far].astype(BF16)
        text_pass_on(text_send3.at[i], text_in3.at[i], 2 - 4 * i, "final")
    join_images(2, 4)
    join_images(1, 2)
    join_images(0, 1)
    wait(image_in2, "sums")
    for h in (0, 1):
        at = slice(h * 32, h * 32 + 32)
        total = image_sum[h] + functools.reduce(jnp.add, [image_in2[h, i].astype(F32) for i in range(3)])
        grads_out[0, at, :] = back_norm(total, si_ref[at, :])
    wait(text_in.at[pl.ds(0, 4)], "final")
    total = text_own[0]
    for ref in (text_in2, text_in3):
        total = total + ref[0].astype(F32) + ref[1].astype(F32)
    grads_out[1] = back_norm(total, st_ref[...])
    wait(rows(img, 0, 960), "leaves", "image")
    wait(rows(txt, 0, 960), "leaves", "text")
    wait(row_in, "leaves", "rows")
    wait(col_in, "leaves", "cols")
    wait(image_send, "leaves", "parts")
    wait(image_send2, "leaves", "sums")
    wait(text_send, "leaves", "joined")
    wait(text_send.at[pl.ds(0, 7)], "leaves", "text sums")


def body(student_image, student_text, teacher_image, teacher_text, teacher_scale, student_scale):
    own, ds = student_image.shape
    width = ds + teacher_image.shape[1]
    vmem = pl.BlockSpec(memory_space=pltpu.VMEM)
    smem = pl.BlockSpec(memory_space=pltpu.SMEM)
    hbm = pl.BlockSpec(memory_space=pltpu.HBM)
    grads = pl.pallas_call(
        kernel,
        out_shape=pltpu.VMEM((2, own, ds), F32),
        in_specs=[smem, smem, hbm, hbm, hbm, hbm],
        out_specs=vmem,
        scratch_shapes=[
            pltpu.VMEM((own, ds), BF16),
            pltpu.VMEM((own, ds), BF16),
            pltpu.VMEM((own, width - ds), BF16),
            pltpu.VMEM((own, width - ds), BF16),
            pltpu.VMEM((1024, width), BF16),
            pltpu.VMEM((1024, width), BF16),
            pltpu.VMEM((1024, 1024), F32),
            pltpu.VMEM((1024, 1024), F32),
            pltpu.VMEM((1024, 1024), BF16),
            pltpu.VMEM((4, 8, 4, 128), F32),
            pltpu.VMEM((8, 2, 1024), F32),
            pltpu.VMEM((3, 16, 128), F32),
            pltpu.VMEM((3, 16, 128), F32),
            pltpu.VMEM((6, 16, 128), F32),
            pltpu.VMEM((8, 16, 128), F32),
            pltpu.VMEM((8, 4, 128), F32),
            pltpu.VMEM((2, 1024), F32),
            pltpu.VMEM((8, 4, 128), F32),
            pltpu.VMEM((2, 1024, 128), F32),
            pltpu.VMEM((2, 1024), F32),
            pltpu.VMEM((2, 1024, 1024), F32),
            pltpu.VMEM((2, 1024, 1024), F32),
            pltpu.VMEM((2, 128, ds), F32),
            pltpu.VMEM((2, 3, 128, ds), BF16),
            pltpu.VMEM((2, 3, 128, ds), BF16),
            pltpu.VMEM((2, 32, ds), F32),
            pltpu.VMEM((2, 3, 32, ds), BF16),
            pltpu.VMEM((2, 3, 32, ds), BF16),
            pltpu.VMEM((NZ, 64, ds), F32),
            pltpu.VMEM((NZ, 64, ds), BF16),
            pltpu.VMEM((NZ, 64, ds), BF16),
            pltpu.VMEM((5, 64, ds), BF16),
            pltpu.VMEM((5, 64, ds), BF16),
            pltpu.VMEM((2, 64, ds), BF16),
            pltpu.VMEM((2, 64, ds), BF16),
            pltpu.SemaphoreType.DMA((SEMAPHORES,)),
        ],
        compiler_params=pltpu.CompilerParams(
            collective_id=0, has_side_effects=True, vmem_limit_bytes=60 * 1024 * 1024
        ),
    )(
        teacher_scale.reshape(1, 1), student_scale.reshape(1, 1),
        student_image, student_text, teacher_image, teacher_text,
    )
    return grads[0] * student_scale, grads[1] * student_scale


def solution(mesh):
    placed = P(("row", "col"), None)
    return jax.shard_map(
        body,
        mesh=mesh,
        in_specs=(placed, placed, placed, placed, P(), P()),
        out_specs=(placed, placed),
        check_vma=False,
    )
```

```python
import functools
import math

import jax
import jax.numpy as jnp
from jax import lax
from jax.experimental import pallas as pl
from jax.experimental.pallas import tpu as pltpu
from jax.sharding import PartitionSpec as P

EPSILON = 1e-12
MESH = pl.DeviceIdType.MESH
NX, NY, NZ = 4, 4, 8
LOG2E = math.log2(math.e)
F32, BF16 = jnp.float32, jnp.bfloat16
SEMAPHORES = 57

PAIRS = (
    ((0, 0), (1, 0)),
    ((3, 0), (0, 1)),
    ((0, 3), (2, 0)),
    ((1, 1), (1, 3)),
    ((3, 1), (3, 3)),
    ((2, 1), (2, 3)),
    ((0, 2), (1, 2)),
    ((3, 2), (2, 2)),
)
HALF_BLOCKS = tuple(tuple((h, p, q) for h in (0, 1) for p, q in pair) for pair in PAIRS)
IMAGE_ROW = {key: g * 128 + k * 32 for g, keys in enumerate(HALF_BLOCKS) for k, key in enumerate(keys)}
TEXT_BLOCKS = (
    (0, 0), (0, 1), (1, 0), (7, 0), (1, 1), (7, 1),
    (2, 0), (6, 0), (2, 1), (6, 1),
    (3, 0), (5, 0), (3, 1), (5, 1),
    (4, 0), (4, 1),
)
TEXT_ROW = {key: i * 64 for i, key in enumerate(TEXT_BLOCKS)}
COLUMNS = ((0, 384), (384, 640), (640, 896), (896, 1024))


def unit_rows(raw):
    values = raw.astype(F32)
    inverse = lax.rsqrt(jnp.sum(values * values, axis=-1, keepdims=True) + EPSILON)
    return values * inverse, inverse


def join_lse(parts):
    top = functools.reduce(jnp.maximum, parts)
    total = functools.reduce(jnp.add, [jnp.exp2(part - top) for part in parts])
    return top + jnp.log(total) * LOG2E


def back_norm(grad, raw):
    unit, inverse = unit_rows(raw)
    return inverse * (grad - unit * jnp.sum(unit * grad, axis=-1, keepdims=True))


def nt_dot(a, b):
    return lax.dot_general(a, b, (((1,), (1,)), ((), ())), preferred_element_type=F32)


def tn_dot(a, b):
    return lax.dot_general(a, b, (((0,), (0,)), ((), ())), preferred_element_type=F32)


def kernel(
    tscale_ref, sscale_ref, si_hbm, st_hbm, ti_hbm, tt_hbm, grads_out,
    si_ref, st_ref, ti_ref, tt_ref, img, txt, teach, learn, weight, row_part, col_part, row_stat, col_stat, row_in, col_in,
    row_local, col_local, row_whole, row_scale, col_scale, by_row, by_col,
    image_own, image_send, image_in, image_sum, image_send2, image_in2,
    text_own, text_send, text_in, text_send2, text_in2, text_send3, text_in3,
    sem,
):
    ds = si_ref.shape[1]
    row, col = lax.axis_index("row"), lax.axis_index("col")
    y, core = row // 2, row % 2
    z, x = col // NX, col % NX

    def device(dx=0, dy=0, dz=0, sibling=False):
        c = 1 - core if sibling else core
        return (((y + dy) % NY) * 2 + c, ((z + dz) % NZ) * NX + (x + dx) % NX)

    def along(half, axis, d):
        return device(dx=d) if (half == 0) == (axis == 1) else device(dy=d)

    names = []

    def semaphore(*name):
        if name not in names:
            names.append(name)
        return sem.at[names.index(name)]

    def send(src, dst, target, leaves, lands):
        pltpu.make_async_remote_copy(
            src_ref=src, dst_ref=dst, send_sem=semaphore("leaves", leaves), recv_sem=semaphore(*lands),
            device_id=target, device_id_type=MESH,
        ).start()

    def wait(ref, *name):
        pltpu.make_async_copy(ref, ref, semaphore(*name)).wait()

    loads = [
        pltpu.make_async_copy(src, dst, semaphore("load", i))
        for i, (src, dst) in enumerate(((tt_hbm, tt_ref), (st_hbm, st_ref), (ti_hbm, ti_ref), (si_hbm, si_ref)))
    ]
    for load in loads:
        load.start()
    barrier = pltpu.get_barrier_semaphore()
    peers = [device(dx=1), device(dx=-1), device(dy=1), device(dy=-1), device(dz=1), device(dz=-1)]
    peers += [device(sibling=True)]
    for peer in peers:
        pl.semaphore_signal(barrier, inc=1, device_id=peer, device_id_type=MESH)
    for load in loads:
        load.wait()

    own_text = TEXT_ROW[(0, 0)]
    for start, size in ((0, 32), (32, 32)):
        for h_ref, lo, hi in ((si_ref, 0, ds), (ti_ref, ds, img.shape[1])):
            at = IMAGE_ROW[(start // 32, 0, 0)]
            img[at : at + size, lo:hi] = unit_rows(h_ref[start : start + size, :])[0].astype(BF16)
    for h_ref, lo, hi in ((st_ref, 0, ds), (tt_ref, ds, img.shape[1])):
        txt[own_text : own_text + 64, lo:hi] = unit_rows(h_ref[...])[0].astype(BF16)

    pl.semaphore_wait(barrier, len(peers))

    def rows(ref, at, size):
        return ref.at[pl.ds(at, size), :]

    def text_rows(k, part, size=16, sib=0):
        return rows(txt, TEXT_ROW[(k, sib)] + part * size, size)

    def image_rows(h, p, q, part=None):
        at = IMAGE_ROW[(h, p, q)]
        return rows(img, at, 32) if part is None else rows(img, at + part * 16, 16)

    def image_on(h, p, q, to, axis, d, lands, part=None):
        send(image_rows(h, p, q, part), image_rows(h, *to, part), along(h, axis, d), "image", lands)

    def to_second_axis(h, p):
        image_on(h, p, 0, (p, 1), 2, -1, ("image", p, 1))
        image_on(h, p, 0, (p, 3), 2, 1, ("image", p, 3))

    def text_on(k, j, part, d, lands):
        send(text_rows(k, part), text_rows(j, part), device(dz=d), "text", lands)

    def text_to_sibling(k, half, lands):
        send(text_rows(k, half, 32), text_rows(k, half, 32, 1), device(sibling=True), "text", ("sibling", lands))

    def text_arrive(k, step):
        wait(rows(txt, 0, 32), "text", k, step)
        for slot, part, d in ((k, step, -1), (NZ - k, 3 - step, 1)):
            if k < 3 or step < 2:
                text_on(slot, slot - d if k < 3 else 4, part, d, ("text", k + 1, step))
            if step % 2:
                text_to_sibling(slot, part // 2, k if k > 1 else 0)

    def text_arrive_last(step):
        wait(rows(txt, 0, 32), "text", 4, step)
        if step == 1:
            for half in (0, 1):
                text_to_sibling(4, half, 4)

    def sibling_arrive(first, blocks):
        wait(rows(txt, 0, blocks * 64), "sibling", first)

    def first_axis_arrive():
        for p, part, d in ((1, 0, -1), (3, 1, 1)):
            wait(rows(img, 0, 64), "image", p, 0)
            for h in (0, 1):
                image_on(h, p, 0, (2, 0), 1, d, ("image", 2, 0), part)
        for p in (1, 3):
            for h in (0, 1):
                to_second_axis(h, p)

    def second_axis_arrive(p):
        for q, part, d in ((1, 0, -1), (3, 1, 1)):
            wait(rows(img, 0, 64), "image", p, q)
            for h in (0, 1):
                image_on(h, p, q, (p, 2), 2, d, ("image", "last"), part)

    teach_scale = tscale_ref[0, 0] * LOG2E
    learn_scale = sscale_ref[0, 0] * LOG2E
    lane = lax.broadcasted_iota(jnp.int32, (128, 128), 1)
    line = lax.broadcasted_iota(jnp.int32, (128, 128), 0)
    spot = line % 32 + 32 * (line // 64)
    learn_spot = lane == spot
    teach_spot = lane == spot + 64

    def logits(first, last, *blocks):
        r = slice(first * 128, last * 128)
        for b in blocks:
            c = slice(*COLUMNS[b])
            for ref, lo, hi, scale in ((learn, 0, ds, learn_scale), (teach, ds, img.shape[1], teach_scale)):
                ref[r, c] = nt_dot(img[r, lo:hi], txt[c, lo:hi]) * scale

        for g in range(first, last):
            r = g * 128
            for b in blocks:
                c = slice(*COLUMNS[b])
                row_ls = []
                for i, ref in enumerate((learn, teach)):
                    block = ref[pl.ds(r, 128), c]
                    top = jnp.max(block, axis=1, keepdims=True)
                    total = jnp.sum(jnp.exp2(block - top), axis=1, keepdims=True)
                    row_ls.append(top + jnp.log(total) * LOG2E)
                    top = jnp.max(block, axis=0, keepdims=True)
                    total = jnp.sum(jnp.exp2(block - top), axis=0, keepdims=True)
                    col_part[g, i : i + 1, c] = top + jnp.log(total) * LOG2E
                packed = jnp.where(learn_spot, row_ls[0], 0.0) + jnp.where(teach_spot, row_ls[1], 0.0)
                row_part[b, g] = jnp.sum(packed.reshape(4, 32, 128), axis=1)

    for step in range(4):
        text_on(0, 1, step, -1, ("text", 1, step))
        text_on(0, 7, 3 - step, 1, ("text", 1, step))
        if step == 0:
            for h in (0, 1):
                image_on(h, 0, 0, (1, 0), 1, -1, ("image", 1, 0))
                image_on(h, 0, 0, (3, 0), 1, 1, ("image", 3, 0))
    for h in (0, 1):
        to_second_axis(h, 0)
    for half in (0, 1):
        text_to_sibling(0, half, 0)

    text_arrive(1, 0)
    first_axis_arrive()
    text_arrive(1, 1)
    text_arrive(1, 2)
    text_arrive(1, 3)
    second_axis_arrive(0)
    wait(rows(img, 0, 64), "image", 2, 0)
    for h in (0, 1):
        to_second_axis(h, 2)
    text_arrive(2, 0)
    sibling_arrive(0, 3)
    logits(0, 3, 0)
    text_arrive(2, 1)
    second_axis_arrive(1)
    text_arrive(2, 2)
    text_arrive(2, 3)
    second_axis_arrive(3)
    text_arrive(3, 0)
    logits(3, 5, 0)
    sibling_arrive(2, 2)
    logits(0, 3, 1)
    text_arrive(3, 1)
    logits(3, 5, 1)
    text_arrive(3, 2)
    second_axis_arrive(2)
    text_arrive(3, 3)
    logits(5, 6, 0, 1)
    text_arrive_last(0)
    sibling_arrive(3, 2)
    logits(0, 6, 2)
    text_arrive_last(1)
    wait(rows(img, 0, 256), "image", "last")
    logits(6, 8, 0, 1, 2)
    sibling_arrive(4, 1)
    logits(0, 8, 3)

    low = lax.broadcasted_iota(jnp.int32, (1, 128), 1) < 64
    half0 = lax.broadcasted_iota(jnp.int32, (1, 128), 1) % 64 < 32
    where_is = {key: (g, k) for g, keys in enumerate(HALF_BLOCKS) for k, key in enumerate(keys)}
    row_places = [
        (((y + dy) % NY) * NX + (x + dx) % NX, where_is[0, dx, dy], where_is[1, dy, dx])
        for dy in range(NY)
        for dx in range(NX)
    ]
    col_places = [(1 - core if sib else core) * NZ + (z + k) % NZ for k, sib in TEXT_BLOCKS]

    def spread(lines):
        lines = jnp.broadcast_to(lines[:, None, :], (4, 32, 128)).reshape(128, 128)
        for mask in (learn_spot, teach_spot):
            yield jnp.broadcast_to(jnp.sum(jnp.where(mask, lines, 0.0), axis=1, keepdims=True), (128, 128))

    col_local[...] = join_lse([col_part[g] for g in range(8)])
    for tile in range(8):
        c = slice(tile * 128, tile * 128 + 128)
        ls, lt = col_local[0:1, c], col_local[1:2, c]
        first, second = col_places[2 * tile : 2 * tile + 2]
        col_stat[0, pl.ds(first, 1), :] = jnp.where(low, ls, pltpu.roll(lt, 64, 1))
        col_stat[0, pl.ds(second, 1), :] = jnp.where(low, pltpu.roll(ls, 64, 1), lt)
    send(col_stat.at[0], col_in.at[0], device(sibling=True), "cols", ("col", 0))
    row_local[...] = join_lse([row_part[b] for b in range(len(COLUMNS))])
    for place, (g0, k0), (g1, k1) in row_places:
        row_stat[0, pl.ds(place, 1), :] = jnp.where(half0, row_local[g0, k0 : k0 + 1, :], row_local[g1, k1 : k1 + 1, :])
    for d in (2, 1, 3):
        send(row_stat.at[0], row_in.at[d - 1], device(dx=d), "rows", ("row", 0))

    def local_softmax(*groups):
        for g in groups:
            r = slice(g * 128, g * 128 + 128)
            row_ls = list(spread(row_local[g]))
            for tile in range(8):
                c = slice(tile * 128, tile * 128 + 128)
                for i, ref in enumerate((learn, teach)):
                    block = ref[r, c] - 1.0
                    by_row[i, r, c] = jnp.exp2(block - row_ls[i])
                    by_col[i, r, c] = jnp.exp2(block - col_local[i : i + 1, c])

    local_softmax(0, 1)
    wait(col_in.at[0], "col", 0)
    col_stat[1] = join_lse([col_stat[0], col_in[0]])
    for d in (4, 3, 5, 2, 6, 1, 7):
        send(col_stat.at[1], col_in.at[d], device(dz=d), "cols", ("col", 1))
    local_softmax(2, 3, 4)
    wait(row_in.at[pl.ds(0, 3)], "row", 0)
    row_stat[1] = join_lse([row_stat[0]] + [row_in[i] for i in range(3)])
    for d in (2, 1, 3):
        send(row_stat.at[1], row_in.at[2 + d], device(dy=d), "rows", ("row", 1))
    local_softmax(5, 6, 7)
    wait(col_in.at[pl.ds(1, NZ - 1)], "col", 1)
    col_stat[2] = join_lse([col_stat[1]] + [col_in[d] for d in range(1, NZ)])
    for tile in range(8):
        c = slice(tile * 128, tile * 128 + 128)
        first, second = col_places[2 * tile : 2 * tile + 2]
        line0 = col_stat[2, pl.ds(first, 1), :]
        line1 = col_stat[2, pl.ds(second, 1), :]
        col_scale[0:1, c] = jnp.exp2(col_local[0:1, c] - jnp.where(low, line0, pltpu.roll(line1, 64, 1)))
        col_scale[1:2, c] = jnp.exp2(col_local[1:2, c] - jnp.where(low, pltpu.roll(line0, 64, 1), line1))
    wait(row_in.at[pl.ds(3, 3)], "row", 1)
    row_stat[2] = join_lse([row_stat[1]] + [row_in[3 + i] for i in range(3)])
    for place, (g0, k0), (g1, k1) in row_places:
        whole = row_stat[2, pl.ds(place, 1), :]
        for g, k in ((g0, k0), (g1, k1)):
            row_whole[g, k : k + 1, :] = whole
    for g in range(8):
        r = slice(g * 128, g * 128 + 128)
        row_scale[0, r, :], row_scale[1, r, :] = spread(jnp.exp2(row_local[g] - row_whole[g]))

    def weights(*tiles):
        for g in range(8):
            r = slice(g * 128, g * 128 + 128)
            learn_row, teach_row = row_scale[0, r, :], row_scale[1, r, :]
            for tile in tiles:
                c = slice(tile * 128, tile * 128 + 128)
                value = (by_row[0, r, c] * learn_row - by_row[1, r, c] * teach_row) + (
                    by_col[0, r, c] * col_scale[0:1, c] - by_col[1, r, c] * col_scale[1:2, c]
                )
                weight[r, c] = value.astype(BF16)

    def text_grads(*tiles):
        c = slice(tiles[0] * 128, tiles[-1] * 128 + 128)
        part = tn_dot(weight[:, c], img[:, :ds])
        for i, (k, sib) in enumerate(TEXT_BLOCKS[2 * tiles[0] : 2 * tiles[-1] + 2]):
            piece = part[i * 64 : i * 64 + 64, :]
            if sib:
                text_send[k] = piece.astype(BF16)
                lands = ("joined", min(k, NZ - k))
                send(text_send.at[k], text_in.at[k], device(sibling=True), "joined", lands)
            else:
                text_own[k] = piece

    def join_cores(*ks):
        for first in sorted({min(k, NZ - k) for k in ks}):
            wait(text_in.at[pl.ds(0, 1 if first in (0, 4) else 2)], "joined", first)
        for k in ks:
            text_own[k] = text_own[k] + text_in[k].astype(F32)

    def image_grads(g):
        r = slice(g * 128, g * 128 + 128)
        part = jnp.dot(weight[r, :], txt[:, :ds], preferred_element_type=F32)
        for k, (h, p, q) in enumerate(HALF_BLOCKS[g]):
            piece = part[k * 32 : k * 32 + 32, :]
            if q == 0:
                image_own[h, p * 32 : p * 32 + 32, :] = piece
            else:
                image_send[h, q - 1, p * 32 : p * 32 + 32, :] = piece.astype(BF16)

    def image_pass_on(q, first, last):
        at = pl.ds(first * 32, (last - first) * 32)
        for h in (0, 1):
            send(image_send.at[h, q - 1, at], image_in.at[h, q - 1, at], along(h, 2, q), "parts", ("parts", first))

    def join_images(first, last):
        wait(image_in.at[:, :, pl.ds(first * 32, (last - first) * 32)], "parts", first)
        for p in range(first, last):
            at = slice(p * 32, p * 32 + 32)
            for h in (0, 1):
                total = image_own[h, at, :] + functools.reduce(
                    jnp.add, [image_in[h, i, at, :].astype(F32) for i in range(3)]
                )
                if p == 0:
                    image_sum[h] = total
                else:
                    image_send2[h, p - 1] = total.astype(BF16)
                    send(image_send2.at[h, p - 1], image_in2.at[h, p - 1], along(h, 1, p), "sums", ("sums",))

    def text_pass_on(src, dst, d, lands):
        send(src, dst, device(dz=d), "text sums", (lands,))

    weights(6, 7)
    text_grads(6, 7)
    weights(5)
    text_grads(5)
    weights(0, 1, 2, 3, 4)
    image_grads(7)
    image_pass_on(2, 2, 4)
    join_cores(3, 5, 4)
    for i, k in ((2, 3), (3, 5), (4, 4)):
        text_send2[i] = text_own[k].astype(BF16)
    for h, d in ((0, 2), (1, -2)):
        at = pl.ds(h * 32, 32)
        text_pass_on(text_send2.at[4, at], text_in2.at[4, at], d, "merge")
    text_pass_on(text_send2.at[2], text_in2.at[2], 1, "merge")
    text_pass_on(text_send2.at[3], text_in2.at[3], -1, "merge")
    image_grads(5)
    image_grads(4)
    image_pass_on(1, 2, 4)
    image_pass_on(3, 2, 4)
    image_grads(6)
    image_pass_on(2, 1, 2)
    image_grads(3)
    image_pass_on(1, 1, 2)
    image_pass_on(3, 1, 2)
    image_pass_on(2, 0, 1)
    image_grads(2)
    image_pass_on(3, 0, 1)
    image_grads(1)
    image_pass_on(1, 0, 1)
    text_grads(1, 2)
    text_grads(3, 4)
    text_grads(0)
    image_grads(0)
    join_cores(1, 7)
    for i, k in ((0, 1), (1, 7)):
        text_send2[i] = text_own[k].astype(BF16)
    text_pass_on(text_send2.at[0], text_in2.at[0], 1, "final")
    text_pass_on(text_send2.at[1], text_in2.at[1], -1, "final")
    join_cores(2, 6)
    join_cores(0)
    wait(text_in2.at[pl.ds(2, 3)], "merge")
    for i, k, h in ((0, 2, 0), (1, 6, 1)):
        joined = text_own[k] + text_in2[2 + i].astype(F32)
        near = slice(h * 32, h * 32 + 32)
        far = slice(32 - h * 32, 64 - h * 32)
        text_send3[i, near, :] = (joined[near] + text_in2[4, near, :].astype(F32)).astype(BF16)
        text_send3[i, far, :] = joined[far].astype(BF16)
        text_pass_on(text_send3.at[i], text_in3.at[i], 2 - 4 * i, "final")
    join_images(2, 4)
    join_images(1, 2)
    join_images(0, 1)
    wait(image_in2, "sums")
    for h in (0, 1):
        at = slice(h * 32, h * 32 + 32)
        total = image_sum[h] + functools.reduce(jnp.add, [image_in2[h, i].astype(F32) for i in range(3)])
        grads_out[0, at, :] = back_norm(total, si_ref[at, :])
    wait(text_in.at[pl.ds(0, 4)], "final")
    total = text_own[0]
    for ref in (text_in2, text_in3):
        total = total + ref[0].astype(F32) + ref[1].astype(F32)
    grads_out[1] = back_norm(total, st_ref[...])
    wait(rows(img, 0, 960), "leaves", "image")
    wait(rows(txt, 0, 960), "leaves", "text")
    wait(row_in, "leaves", "rows")
    wait(col_in, "leaves", "cols")
    wait(image_send, "leaves", "parts")
    wait(image_send2, "leaves", "sums")
    wait(text_send, "leaves", "joined")
    wait(text_send.at[pl.ds(0, 7)], "leaves", "text sums")


def body(student_image, student_text, teacher_image, teacher_text, teacher_scale, student_scale):
    own, ds = student_image.shape
    width = ds + teacher_image.shape[1]
    vmem = pl.BlockSpec(memory_space=pltpu.VMEM)
    smem = pl.BlockSpec(memory_space=pltpu.SMEM)
    hbm = pl.BlockSpec(memory_space=pltpu.HBM)
    grads = pl.pallas_call(
        kernel,
        out_shape=pltpu.VMEM((2, own, ds), F32),
        in_specs=[smem, smem, hbm, hbm, hbm, hbm],
        out_specs=vmem,
        scratch_shapes=[
            pltpu.VMEM((own, ds), BF16),
            pltpu.VMEM((own, ds), BF16),
            pltpu.VMEM((own, width - ds), BF16),
            pltpu.VMEM((own, width - ds), BF16),
            pltpu.VMEM((1024, width), BF16),
            pltpu.VMEM((1024, width), BF16),
            pltpu.VMEM((1024, 1024), F32),
            pltpu.VMEM((1024, 1024), F32),
            pltpu.VMEM((1024, 1024), BF16),
            pltpu.VMEM((4, 8, 4, 128), F32),
            pltpu.VMEM((8, 2, 1024), F32),
            pltpu.VMEM((3, 16, 128), F32),
            pltpu.VMEM((3, 16, 128), F32),
            pltpu.VMEM((6, 16, 128), F32),
            pltpu.VMEM((8, 16, 128), F32),
            pltpu.VMEM((8, 4, 128), F32),
            pltpu.VMEM((2, 1024), F32),
            pltpu.VMEM((8, 4, 128), F32),
            pltpu.VMEM((2, 1024, 128), F32),
            pltpu.VMEM((2, 1024), F32),
            pltpu.VMEM((2, 1024, 1024), F32),
            pltpu.VMEM((2, 1024, 1024), F32),
            pltpu.VMEM((2, 128, ds), F32),
            pltpu.VMEM((2, 3, 128, ds), BF16),
            pltpu.VMEM((2, 3, 128, ds), BF16),
            pltpu.VMEM((2, 32, ds), F32),
            pltpu.VMEM((2, 3, 32, ds), BF16),
            pltpu.VMEM((2, 3, 32, ds), BF16),
            pltpu.VMEM((NZ, 64, ds), F32),
            pltpu.VMEM((NZ, 64, ds), BF16),
            pltpu.VMEM((NZ, 64, ds), BF16),
            pltpu.VMEM((5, 64, ds), BF16),
            pltpu.VMEM((5, 64, ds), BF16),
            pltpu.VMEM((2, 64, ds), BF16),
            pltpu.VMEM((2, 64, ds), BF16),
            pltpu.SemaphoreType.DMA((SEMAPHORES,)),
        ],
        compiler_params=pltpu.CompilerParams(
            collective_id=0, has_side_effects=True, vmem_limit_bytes=60 * 1024 * 1024
        ),
    )(
        teacher_scale.reshape(1, 1), student_scale.reshape(1, 1),
        student_image, student_text, teacher_image, teacher_text,
    )
    return grads[0] * student_scale, grads[1] * student_scale


def solution(mesh):
    placed = P(("row", "col"), None)
    return jax.shard_map(
        body,
        mesh=mesh,
        in_specs=(placed, placed, placed, placed, P(), P()),
        out_specs=(placed, placed),
        check_vma=False,
    )
```
